32 devices in a mesh: groups: 2 (over y), blk: 4 (over z), sub: 2 (over x), lev: 2 (over core).
Axes of the slice: x: 2, y: 2, z: 4, core: 2. Of those that a mesh axis runs over, the one named last changes fastest.
Arguments:
- ocean_forcing: float32 [4, 512, 4, 8, 128], P(('groups', 'sub'), 'blk'), parts along dimension 0, may hold values from -6 to 6
- ice_home: int32 [4, 512], P(('groups', 'sub'), 'blk'), parts along dimension 0, may hold values from -1 to 383, as said below
- ice_velocity: float32 [4, 384, 2, 8, 128], P(('groups', 'sub'), 'blk'), parts along dimension 0, may hold values from -3 to 3
- ice_stress: float32 [4, 384, 3, 8, 128], P(('groups', 'sub'), 'blk'), parts along dimension 0, may hold values from -3 to 3
- ice_area: float32 [4, 384, 4, 8, 128], P(('groups', 'sub'), 'blk', 'lev'), parts along dimension 0, may hold values from 0 to 0.24
- ice_thick: float32 [4, 384, 4, 8, 128], P(('groups', 'sub'), 'blk', 'lev'), parts along dimension 0, may hold values from 0.2 to 4
- neighbors: int32 [4, 384, 6], P(('groups', 'sub'), 'blk'), parts along dimension 0, may hold values from -1 to 767, as said below
Outputs:
- ocean_stress: float32 [4, 512, 2, 8, 128], P(('groups', 'sub'), 'blk'), parts along dimension 0
- final_velocity: float32 [4, 384, 2, 8, 128], P(('groups', 'sub'), 'blk'), parts along dimension 0
- final_stress: float32 [4, 384, 3, 8, 128], P(('groups', 'sub'), 'blk'), parts along dimension 0
The draws below stay inside these ranges and needn't reach their ends.
There are 2 independent parts, one for each index of `groups`. The reference program is written for one: setup_inputs(seed, part) draws one part's arguments, and reference() takes and returns one part's arrays. A program takes and returns all parts, laid end to end along the dimension named above; each array names one. Nothing has to cross between parts.
Inputs may be any that keep to these rules, and one draw needn't show every extreme that they name: `ice_home`: sector q holds the block columns q * 4 to q * 4 + 3 of the grid; its block b lies in block row b // 4, column b % 4. The blocks with ice of a sector, numbered k = 0, 1, ... in block order, are dealt in runs of 4: run r = k // 4 lies in pass p = r // 4 at place m = r % 4, and goes to owner m along blk in even passes and 3 - m in odd ones, slot p * 4 + k % 4; the entry is owner * 96 + slot; -1 marks a block without ice. Each sector has exactly 384 blocks with ice, all in its first 97 block rows. `neighbors`: entry d of an ice block names the ice block beside it: d = 0 the next block row, 1 the next block column, 2 the previous row, 3 the previous column, 4 the previous row and next column, 5 the next row and previous column (columns run on across sectors), as (o * 2 + q) * 96 + s for owner o, sector q, slot s; -1 where that block has no ice or lies outside the grid. A named block's owner differs from the block's own by at most one along blk, and its sector by at most one. The last slot of the last owner in the last sector is always named by some entry.
All inputs are finite; a program needn't handle non-finite values.
Results may differ from the reference program's by a relative error of at most 0.0003.
Values sent between devices are 32-bit elements; how exact they have to be, the bound alone decides.
A program may use at most 128 MiB of HBM per device.

```python
import math
import jax
import jax.numpy as jnp
from jax import lax

BX = 8
BY = 128
SCOLS = 4
NCAT = 4
ITERS = 4
SECTORS = 2
OWNERS = 4
SECT_BLOCKS = 512
SLOTS = 96
ICE_BLOCKS = 384
BROWS = 128
N_BLK = 4


def ice_layout(key, part):
    key = jax.random.fold_in(key, part)
    band_start = SLOTS * N_BLK // SCOLS - 1
    scores = jax.random.randint(key, (SECTORS, 2 * SCOLS), 0, 2 ** 20) * (2 * SCOLS) + jnp.arange(2 * SCOLS, dtype=jnp.int32)[None, :]
    chosen = lax.top_k(scores, SCOLS)[1]
    band = jnp.any(chosen[:, :, None] == jnp.arange(2 * SCOLS, dtype=jnp.int32)[None, None, :], axis=1)
    block = jnp.arange(SECT_BLOCKS, dtype=jnp.int32)
    offset = jnp.clip(block - band_start * SCOLS, 0, 2 * SCOLS - 1)
    in_band = (block >= band_start * SCOLS) & (block < (band_start + 2) * SCOLS)
    iced = (block < band_start * SCOLS)[None, :] | in_band[None, :] & band[:, offset]
    ranked = jnp.cumsum(iced.astype(jnp.int32), axis=1) - 1
    run_index = ranked // SCOLS
    pass_index = run_index // N_BLK
    place = run_index % N_BLK
    owner = jnp.where(pass_index % 2 == 0, place, N_BLK - 1 - place)
    slot_index = pass_index * SCOLS + ranked % SCOLS
    home = jnp.where(iced, owner * SLOTS + slot_index, -1).astype(jnp.int32)
    sector = jnp.arange(SECTORS, dtype=jnp.int32)[:, None]
    global_id = jnp.where(iced, (owner * SECTORS + sector) * SLOTS + slot_index, -1).astype(jnp.int32)
    layout = global_id.reshape(SECTORS, BROWS, SCOLS).transpose(1, 0, 2).reshape(BROWS, SECTORS * SCOLS)
    padded = jnp.pad(layout, 1, constant_values=-1)
    beside = jnp.stack([padded[2:, 1:-1], padded[1:-1, 2:], padded[:-2, 1:-1], padded[1:-1, :-2], padded[:-2, 2:], padded[2:, :-2]], axis=-1)
    per_block = beside.reshape(BROWS, SECTORS, SCOLS, 6).transpose(1, 0, 2, 3).reshape(SECTORS, SECT_BLOCKS, 6)
    target = jnp.where(iced, home, ICE_BLOCKS).astype(jnp.int32)
    sector_rows = jnp.broadcast_to(sector, target.shape)
    table = jnp.full((SECTORS, ICE_BLOCKS + 1, 6), -1, jnp.int32).at[sector_rows, target].set(per_block)[:, :ICE_BLOCKS]
    return (home, table)


def draw_ice_home(key, part):
    return ice_layout(key, part)[0]


def draw_neighbors(key, part):
    return ice_layout(key, part)[1]


def shard_levels(own_key, dims, shards, least, largest):
    level, own = 1.0, jax.random.fold_in(own_key, 6)
    for axis_at, parts in shards:
        steps = jnp.exp(jax.random.uniform(jax.random.fold_in(own, axis_at), (parts,), jnp.float32, least / len(shards), largest / len(shards)))
        level = level * jnp.repeat(steps, dims[axis_at] // parts).reshape([-1 if axis == axis_at else 1 for axis in range(len(dims))])
    return level


def bell_draw(own_key, dims, scale, limit, shards=(), kind=jnp.bfloat16):
    result = jax.random.normal(own_key, dims, jnp.float32) * scale
    if len(shards) > 0:
        result = shard_levels(own_key, dims, shards, -0.22, 0.18) * result
    return jnp.clip(result, min=-limit, max=limit).astype(kind)


def setup_inputs(seed: int = 0, part: int = 0) -> dict:
    splits = jax.random.split(jax.random.key(seed), 8)
    own_keys = jax.random.split(jax.random.fold_in(splits[7], part), 8)
    ocean_forcing = bell_draw(own_keys[0], (SECTORS, SECT_BLOCKS, 4, BX, BY), 1.0, 6.0, ((0, 2), (1, 4)), jnp.float32)
    ice_home = draw_ice_home(jax.random.fold_in(jax.random.fold_in(splits[7], part), 71), part)
    ice_velocity = bell_draw(own_keys[2], (SECTORS, ICE_BLOCKS, 2, BX, BY), 0.5, 3.0, ((0, 2), (1, 4)), jnp.float32)
    ice_stress = bell_draw(own_keys[3], (SECTORS, ICE_BLOCKS, 3, BX, BY), 0.5, 3.0, ((0, 2), (1, 4)), jnp.float32)
    ice_area = jnp.clip(0.24 * jax.random.uniform(own_keys[4], (SECTORS, ICE_BLOCKS, NCAT, BX, BY), jnp.float32) ** shard_levels(own_keys[4], (SECTORS, ICE_BLOCKS, NCAT, BX, BY), ((0, 2), (1, 4), (2, 2)), -0.2, 0.2), 0.0, 0.24)
    ice_thick = jnp.clip(jnp.exp(math.log(4.0) - 2.9957323 * jax.random.uniform(own_keys[5], (SECTORS, ICE_BLOCKS, NCAT, BX, BY), jnp.float32) ** shard_levels(own_keys[5], (SECTORS, ICE_BLOCKS, NCAT, BX, BY), ((0, 2), (1, 4), (2, 2)), -0.2, 0.2)), 0.2, 4.0)
    neighbors = draw_neighbors(jax.random.fold_in(jax.random.fold_in(splits[7], part), 71), part)
    return dict(ocean_forcing=ocean_forcing, ice_home=ice_home, ice_velocity=ice_velocity, ice_stress=ice_stress, ice_area=ice_area, ice_thick=ice_thick, neighbors=neighbors)


strength_scale = 4.0
cover_decay = 4.0
elastic_weight = 1.0
ellipse_square = 4.0
delta_floor = 0.05
inertia = 2.0
speed_floor = 0.2
coriolis = 0.6

def stress_step(sigma_one, sigma_two, sigma_shear, strength, flow_x, next_x_of_x, next_y_of_x, flow_y, next_x_of_y, next_y_of_y):
    stretch_x = next_x_of_x - flow_x
    stretch_y = next_y_of_y - flow_y
    shear_rate = next_y_of_x - flow_x + (next_x_of_y - flow_y)
    divergence = stretch_x + stretch_y
    tension = stretch_x - stretch_y
    delta = jnp.sqrt(divergence * divergence + (tension * tension + shear_rate * shear_rate) / ellipse_square + delta_floor * delta_floor)
    weight = elastic_weight * strength / delta
    relax_total = 1.0 + elastic_weight
    new_one = (sigma_one + weight * divergence - elastic_weight * strength) / relax_total
    new_two = (sigma_two + weight * tension / ellipse_square) / relax_total
    new_shear = (sigma_shear + weight * shear_rate / (2.0 * ellipse_square)) / relax_total
    return (new_one, new_two, new_shear)

def stress_force(sigma_one, sigma_two, sigma_shear, upper_normal, upper_shear, left_shear, left_normal):
    normal_x = 0.5 * (sigma_one + sigma_two)
    normal_y = 0.5 * (sigma_one - sigma_two)
    above_normal = jnp.concatenate([upper_normal[:, None, :], normal_x[:, :-1, :]], axis=1)
    above_shear = jnp.concatenate([upper_shear[:, None, :], sigma_shear[:, :-1, :]], axis=1)
    before_shear = jnp.concatenate([left_shear[:, :, None], sigma_shear[:, :, :-1]], axis=2)
    before_normal = jnp.concatenate([left_normal[:, :, None], normal_y[:, :, :-1]], axis=2)
    force_x = normal_x - above_normal + (sigma_shear - before_shear)
    force_y = sigma_shear - above_shear + (normal_y - before_normal)
    return (force_x, force_y)

def water_drag_of(flow_x, flow_y, forcing):
    slip_x = forcing[:, 2] - flow_x
    slip_y = forcing[:, 3] - flow_y
    return jnp.sqrt(slip_x * slip_x + slip_y * slip_y + speed_floor * speed_floor)

def momentum_step(flow_x, flow_y, force_x, force_y, mass, forcing):
    water_drag = water_drag_of(flow_x, flow_y, forcing)
    diagonal = mass * inertia + water_drag
    rotation = mass * coriolis
    right_x = mass * inertia * flow_x + force_x + forcing[:, 0] + water_drag * forcing[:, 2]
    right_y = mass * inertia * flow_y + force_y + forcing[:, 1] + water_drag * forcing[:, 3]
    determinant = diagonal * diagonal + rotation * rotation
    return ((diagonal * right_x + rotation * right_y) / determinant, (diagonal * right_y - rotation * right_x) / determinant)

def ocean_share(flow_x, flow_y, area, forcing):
    water_drag = water_drag_of(flow_x, flow_y, forcing)
    stress_x = area * water_drag * (forcing[:, 2] - flow_x) + (1.0 - area) * forcing[:, 0]
    stress_y = area * water_drag * (forcing[:, 3] - flow_y) + (1.0 - area) * forcing[:, 1]
    return jnp.stack([stress_x, stress_y], axis=1)

def flatten_ice(array):
    rest = array.shape[2:]
    grouped = array.reshape((SECTORS, OWNERS, SLOTS) + rest)
    return jnp.swapaxes(grouped, 0, 1).reshape((OWNERS * SECTORS * SLOTS,) + rest)

def restore_ice(array):
    rest = array.shape[1:]
    grouped = array.reshape((OWNERS, SECTORS, SLOTS) + rest)
    return jnp.swapaxes(grouped, 0, 1).reshape((SECTORS, OWNERS * SLOTS) + rest)

def lookup(edges, global_id):
    safe = jnp.clip(global_id, 0, edges.shape[0] - 1)
    fetched = edges[safe]
    present = (global_id >= 0).reshape((-1,) + (1,) * (edges.ndim - 1))
    return jnp.where(present, fetched, jnp.zeros_like(fetched))

def reference(ocean_forcing, ice_home, ice_velocity, ice_stress, ice_area, ice_thick, neighbors):
    sector_index = jnp.broadcast_to(jnp.arange(SECTORS, dtype=jnp.int32)[:, None], ice_home.shape)
    target = jnp.where(ice_home >= 0, ice_home, ICE_BLOCKS).astype(jnp.int32)
    placed = jnp.zeros((SECTORS, ICE_BLOCKS + 1) + ocean_forcing.shape[2:], ocean_forcing.dtype)
    placed = placed.at[sector_index, target].set(ocean_forcing)[:, :ICE_BLOCKS]
    forcing = flatten_ice(placed)
    table = flatten_ice(neighbors)
    area = flatten_ice(lax.optimization_barrier(jnp.sum(ice_area, axis=2)))
    volume = flatten_ice(lax.optimization_barrier(jnp.sum(ice_area * ice_thick, axis=2)))
    strength = strength_scale * volume * jnp.exp(-cover_decay * (1.0 - area))
    mass = volume
    velocity = flatten_ice(ice_velocity)
    stress = flatten_ice(ice_stress)
    flow_x, flow_y = (velocity[:, 0], velocity[:, 1])
    sigma_one, sigma_two, sigma_shear = (stress[:, 0], stress[:, 1], stress[:, 2])
    for sweep in range(ITERS):
        row_x = lookup(flow_x[:, 0, :], table[:, 0])
        row_y = lookup(flow_y[:, 0, :], table[:, 0])
        col_x = lookup(flow_x[:, :, 0], table[:, 1])
        col_y = lookup(flow_y[:, :, 0], table[:, 1])
        next_x_of_x = jnp.concatenate([flow_x[:, 1:, :], row_x[:, None, :]], axis=1)
        next_x_of_y = jnp.concatenate([flow_y[:, 1:, :], row_y[:, None, :]], axis=1)
        next_y_of_x = jnp.concatenate([flow_x[:, :, 1:], col_x[:, :, None]], axis=2)
        next_y_of_y = jnp.concatenate([flow_y[:, :, 1:], col_y[:, :, None]], axis=2)
        sigma_one, sigma_two, sigma_shear = stress_step(sigma_one, sigma_two, sigma_shear, strength, flow_x, next_x_of_x, next_y_of_x, flow_y, next_x_of_y, next_y_of_y)
        normal_x = 0.5 * (sigma_one + sigma_two)
        normal_y = 0.5 * (sigma_one - sigma_two)
        upper_normal = lookup(normal_x[:, -1, :], table[:, 2])
        upper_shear = lookup(sigma_shear[:, -1, :], table[:, 2])
        left_shear = lookup(sigma_shear[:, :, -1], table[:, 3])
        left_normal = lookup(normal_y[:, :, -1], table[:, 3])
        force_x, force_y = stress_force(sigma_one, sigma_two, sigma_shear, upper_normal, upper_shear, left_shear, left_normal)
        flow_x, flow_y = momentum_step(flow_x, flow_y, force_x, force_y, mass, forcing)
    blended = restore_ice(ocean_share(flow_x, flow_y, area, forcing))
    safe_home = jnp.clip(ice_home, 0, ICE_BLOCKS - 1).astype(jnp.int32)
    fetched = blended[sector_index, safe_home]
    ocean_stress = jnp.where((ice_home >= 0)[:, :, None, None, None], fetched, ocean_forcing[:, :, 0:2])
    final_velocity = restore_ice(jnp.stack([flow_x, flow_y], axis=1))
    final_stress = restore_ice(jnp.stack([sigma_one, sigma_two, sigma_shear], axis=1))
    return (ocean_stress, final_velocity, final_stress)
```

```python
import functools

import jax
import jax.numpy as jnp
from jax import lax
from jax.experimental import pallas as pl
from jax.experimental.pallas import tpu as pltpu
from jax.sharding import PartitionSpec as P

SCOLS = 4
ITERS = 4
UNROLL = 4

strength_scale = 4.0
cover_decay = 4.0
elastic_weight = 1.0
ellipse_square = 4.0
delta_floor = 0.05
inertia = 2.0
speed_floor = 0.2
coriolis = 0.6

MESH = pl.DeviceIdType.MESH


def kernel(
    owners,
    sectors,
    src_ref,
    lane_ref,
    row_ref,
    beside_ref,
    ocean_ref,
    vel_in,
    stress_in,
    area_in,
    thick_in,
    ocean_out,
    vel,
    sig,
    send_buf,
    edge_send,
    forcing,
    edge_land,
    cover,
    area_buf,
    mass_buf,
    strength_buf,
    blend,
    back,
    vel_sec,
    vel_cross,
    str_sec,
    str_cross,
    pick_vel,
    pick_str,
    out_send,
    out_recv,
    edge_sems,
    fwd_send,
    fwd_recv,
    cover_sems,
    halo_send,
    halo_recv,
    ret_send,
    ret_recv,
    ret_edge,
    back_send,
    back_recv,
):
    group = lax.axis_index("groups")
    me = lax.axis_index("blk")
    sector = lax.axis_index("sub")
    lev = lax.axis_index("lev")
    slots = vel.shape[0]
    blocks = ocean_ref.shape[0]
    cap = blocks // owners
    chunks = slots // cap
    section = vel_sec.shape[0] // 4
    f32 = jnp.float32

    def at(blk, sub=None, core=None):
        return (
            group,
            blk,
            sector if sub is None else sub,
            lev if core is None else core,
        )

    partner = at(me, None, 1 - lev)

    def remote(src, dst, send, recv, target):
        return pltpu.make_async_remote_copy(
            src_ref=src,
            dst_ref=dst,
            send_sem=send,
            recv_sem=recv,
            device_id=target,
            device_id_type=MESH,
        )

    lanes = lax.broadcasted_iota(jnp.int32, (8, 128), 1)
    subs = lax.broadcasted_iota(jnp.int32, (8, 128), 0)
    zero = jnp.zeros((8, 128), f32)

    for sec in (vel_sec, str_sec):
        for a in range(3):
            sec[a * section + 2 * slots : (a + 1) * section, :] = jnp.zeros((16, 128), f32)
        sec[3 * section :, :] = jnp.zeros((section, 128), f32)
    vel_cross[...] = jnp.zeros_like(vel_cross)
    str_cross[...] = jnp.zeros_like(str_cross)

    barrier = pltpu.get_barrier_semaphore()

    def greet(target):
        pl.semaphore_signal(barrier, inc=1, device_id=target, device_id_type=MESH)

    greet(partner)
    for delta in range(1, owners):
        greet(at(lax.rem(me + delta, owners)))
    expected = owners
    for ds in (-1, 1):
        for da in (-1, 0, 1):
            q, o = sector + ds, me + da
            ok = (q >= 0) & (q < sectors) & (o >= 0) & (o < owners)

            @pl.when(ok)
            def _():
                greet(at(o, q))

            expected = expected + ok.astype(jnp.int32)
    pl.semaphore_wait(barrier, expected)

    def out_copy(o, s):
        return remote(
            send_buf.at[o],
            forcing.at[lev, pl.ds(s * cap, cap)],
            out_send.at[o],
            out_recv.at[s],
            at(o),
        )

    full = me * cap < slots
    for delta in list(range(1, owners)):
        o = lax.rem(me + delta, owners)

        @pl.when(full)
        def _():
            def fill(j, c):
                src = src_ref[o * cap + j]
                safe = jnp.maximum(src, 0)
                for f in range(2):
                    tile = ocean_ref[safe, 2 * lev + f]
                    send_buf[o, j, f] = jnp.where(src >= 0, tile, 0.0)
                return c

            lax.fori_loop(0, cap, fill, 0, unroll=UNROLL)
            out_copy(o, me).start()

    def edge_owner(s):
        last_pass = s * (cap // SCOLS) - 1
        return jnp.where(lax.rem(last_pass + 2, 2) == 0, owners - 1, 0)

    def has_edge(s):
        return (s >= 1) & (s <= chunks)

    def edge_copy(s, o):
        return remote(
            edge_send, edge_land.at[s], edge_sems.at[0], edge_sems.at[1 + s], at(o)
        )

    @pl.when(has_edge(me))
    def _():
        for j in range(SCOLS):
            src = src_ref[blocks + j]
            safe = jnp.maximum(src, 0)
            for f in range(4):
                edge_send[j, f] = jnp.where(src >= 0, ocean_ref[safe, f], 0.0)
        edge_copy(me, edge_owner(me)).start()

    def halo_copies(sec, cross, down, base):
        mine = sec.at[pl.ds(section, section)]
        cols = sec.at[pl.ds(section + 2 * slots, 16)]
        made = []
        made.append((me + 1 < owners, remote(
            mine, sec.at[pl.ds(0, section)], halo_send.at[base], halo_recv.at[base],
            at(me + 1)), me >= 1))
        made.append((me >= 1, remote(
            mine, sec.at[pl.ds(2 * section, section)], halo_send.at[base + 1],
            halo_recv.at[base + 1], at(me - 1)), me + 1 < owners))
        target = sector + down
        source = sector - down
        t_ok = (target >= 0) & (target < sectors)
        s_ok = (source >= 0) & (source < sectors)
        for i, da in enumerate((1, 0, -1)):
            o, p = me + da, me - da
            made.append((t_ok & (o >= 0) & (o < owners), remote(
                cols, cross.at[1 - da], halo_send.at[base + 2 + i],
                halo_recv.at[base + 2 + i], at(o, target)),
                s_ok & (p >= 0) & (p < owners)))
        return made

    vel_halo = halo_copies(vel_sec, vel_cross, -1, 0)
    str_halo = halo_copies(str_sec, str_cross, 1, 5)

    def halo_start(copies):
        for ok, copy, _ in copies:
            pl.when(ok)(copy.start)

    def halo_wait(copies):
        for ok, copy, arriving in copies:
            pl.when(arriving)(copy.wait_recv)
            pl.when(ok)(copy.wait_send)

    def pack(sec, j, row_a, row_b):
        sec[pl.ds(section + j, 1), :] = row_a
        sec[pl.ds(section + slots + j, 1), :] = row_b

    def put_cols(sec, cols):
        sec[section + 2 * slots : section + 2 * slots + 8, :] = cols[0]
        sec[section + 2 * slots + 8 : section + 2 * slots + 16, :] = cols[1]

    def pack_velocity(j, cols, x, y):
        pack(vel_sec, j, x[0:1], y[0:1])
        here = lanes == j
        return (
            jnp.where(here, x[:, 0:1], cols[0]),
            jnp.where(here, y[:, 0:1], cols[1]),
        )

    def start_body(j, cols):
        x, y = vel_in[j, 0], vel_in[j, 1]
        vel[j, 0] = x
        vel[j, 1] = y
        return pack_velocity(j, cols, x, y)

    cols = lax.fori_loop(0, slots, start_body, (zero, zero), unroll=UNROLL)
    put_cols(vel_sec, cols)
    halo_start(vel_halo)

    def part_body(j, c):
        first, second = area_in[j, 0], area_in[j, 1]
        cover[0, 0, j] = first + second
        cover[0, 1, j] = first * thick_in[j, 0] + second * thick_in[j, 1]
        return c

    lax.fori_loop(0, slots, part_body, 0, unroll=UNROLL)
    cover_copy = remote(
        cover.at[0], cover.at[1], cover_sems.at[0], cover_sems.at[1], partner
    )
    cover_copy.start()

    @pl.when(full)
    def _():
        def fill(j, c):
            src = src_ref[me * cap + j]
            safe = jnp.maximum(src, 0)
            for f in range(4):
                tile = ocean_ref[safe, f]
                forcing[f // 2, me * cap + j, f % 2] = jnp.where(src >= 0, tile, 0.0)
            return c

        lax.fori_loop(0, cap, fill, 0, unroll=UNROLL)

    spot = lax.broadcasted_iota(jnp.int32, (128, 128), 0)
    for beside, d, toward in ((pick_vel, 1, 1), (pick_str, 3, -1)):
        ids = beside_ref[d : d + 1, :]
        for i in range(6):
            across, aside = i % 3 - 1, (i // 3) * toward
            base = ((me + across) * sectors + sector + aside) * slots
            hit = (ids - base == spot) & (spot < slots) & (ids >= 0)
            beside[i * 128 : (i + 1) * 128, :] = hit.astype(f32).astype(jnp.bfloat16)

    def fetch_columns(sec, cross, pick):
        parts = [
            sec[a * section + 2 * slots : (a + 1) * section, :] for a in range(3)
        ] + [cross[a] for a in range(3)]
        whole = jnp.concatenate(parts, axis=1)
        first = whole.astype(jnp.bfloat16)
        rest = whole - first.astype(f32)
        second = rest.astype(jnp.bfloat16)
        third = (rest - second.astype(f32)).astype(jnp.bfloat16)
        terms = jnp.concatenate([first, second, third], axis=0)
        got = jnp.dot(terms, pick[...], preferred_element_type=f32)
        got = got[0:16] + got[16:32] + got[32:48]
        return got[0:8], got[8:16]

    cover_copy.wait()

    def cover_body(j, c):
        area = cover[0, 0, j] + cover[1, 0, j]
        volume = cover[0, 1, j] + cover[1, 1, j]
        area_buf[j] = area
        mass_buf[j] = volume
        strength_buf[j] = strength_scale * volume * jnp.exp(-cover_decay * (1.0 - area))
        return c

    lax.fori_loop(0, slots, cover_body, 0, unroll=UNROLL)

    def fwd_copy(s, half):
        place = forcing.at[half, pl.ds(s * cap, cap)]
        return remote(place, place, fwd_send.at[s], fwd_recv.at[s], partner)

    def ret_copy(s, o):
        return remote(
            blend.at[lev, pl.ds(s * cap, cap)],
            back.at[lev, pl.ds(o * cap, cap)],
            ret_send.at[s],
            ret_recv.at[o],
            at(s),
        )

    def ret_edge_copy(s):
        return remote(
            blend.at[:, pl.ds(s * cap - SCOLS, SCOLS)],
            back.at[:, pl.ds(blocks, SCOLS)],
            ret_edge.at[1 + s],
            ret_edge.at[0],
            at(s),
        )

    for sweep in range(ITERS):
        source = stress_in if sweep == 0 else sig
        halo_wait(vel_halo)
        right_x, right_y = fetch_columns(vel_sec, vel_cross, pick_vel)

        def stress_body(j, cols):
            x, y = vel[j, 0], vel[j, 1]
            place = row_ref[j]
            below_x = vel_sec[pl.ds(place, 1), :]
            below_y = vel_sec[pl.ds(place + slots, 1), :]
            last_row, last_col = subs == 7, lanes == 127
            next_x_of_x = jnp.where(last_row, below_x, pltpu.roll(x, 7, 0))
            next_x_of_y = jnp.where(last_row, below_y, pltpu.roll(y, 7, 0))
            turn = 127 - j
            next_y_of_x = jnp.where(last_col, pltpu.roll(right_x, turn, 1), pltpu.roll(x, 127, 1))
            next_y_of_y = jnp.where(last_col, pltpu.roll(right_y, turn, 1), pltpu.roll(y, 127, 1))
            strength = strength_buf[j]
            stretch_x = next_x_of_x - x
            stretch_y = next_y_of_y - y
            shear_rate = next_y_of_x - x + (next_x_of_y - y)
            divergence = stretch_x + stretch_y
            tension = stretch_x - stretch_y
            square = (
                divergence * divergence
                + (tension * tension + shear_rate * shear_rate) * (1.0 / ellipse_square)
                + delta_floor * delta_floor
            )
            weight = elastic_weight * strength * lax.rsqrt(square)
            relax = 1.0 / (1.0 + elastic_weight)
            one = (source[j, 0] + weight * divergence - elastic_weight * strength) * relax
            two = (source[j, 1] + weight * tension * (1.0 / ellipse_square)) * relax
            shear = (source[j, 2] + weight * shear_rate * (0.5 / ellipse_square)) * relax
            sig[j, 0] = one
            sig[j, 1] = two
            sig[j, 2] = shear
            normal_x = 0.5 * (one + two)
            normal_y = 0.5 * (one - two)
            pack(str_sec, j, normal_x[7:8], shear[7:8])
            here = lanes == j
            return (
                jnp.where(here, shear[:, 127:128], cols[0]),
                jnp.where(here, normal_y[:, 127:128], cols[1]),
            )

        cols = lax.fori_loop(0, slots, stress_body, (zero, zero), unroll=UNROLL)
        put_cols(str_sec, cols)
        halo_start(str_halo)
        halo_wait(str_halo)
        left_shear, left_normal = fetch_columns(str_sec, str_cross, pick_str)

        final = sweep == ITERS - 1

        def flow_body(j, cols):
            x, y = vel[j, 0], vel[j, 1]
            one, two, shear = sig[j, 0], sig[j, 1], sig[j, 2]
            normal_x = 0.5 * (one + two)
            normal_y = 0.5 * (one - two)
            place = row_ref[slots + j]
            above_n = str_sec[pl.ds(place, 1), :]
            above_s = str_sec[pl.ds(place + slots, 1), :]
            first_row, first_col = subs == 0, lanes == 0
            turn = 128 - j
            turn = jnp.where(turn == 128, 0, turn)
            above_normal = jnp.where(first_row, above_n, pltpu.roll(normal_x, 1, 0))
            above_shear = jnp.where(first_row, above_s, pltpu.roll(shear, 1, 0))
            before_shear = jnp.where(
                first_col, pltpu.roll(left_shear, turn, 1), pltpu.roll(shear, 1, 1)
            )
            before_normal = jnp.where(
                first_col, pltpu.roll(left_normal, turn, 1), pltpu.roll(normal_y, 1, 1)
            )
            force_x = normal_x - above_normal + (shear - before_shear)
            force_y = shear - above_shear + (normal_y - before_normal)
            wind_x, wind_y = forcing[0, j, 0], forcing[0, j, 1]
            cur_x, cur_y = forcing[1, j, 0], forcing[1, j, 1]
            slip_x, slip_y = cur_x - x, cur_y - y
            drag = jnp.sqrt(slip_x * slip_x + slip_y * slip_y + speed_floor * speed_floor)
            mass = mass_buf[j]
            heavy = mass * inertia
            diagonal = heavy + drag
            rotation = mass * coriolis
            rhs_x = heavy * x + force_x + wind_x + drag * cur_x
            rhs_y = heavy * y + force_y + wind_y + drag * cur_y
            inverse = 1.0 / (diagonal * diagonal + rotation * rotation)
            x = (diagonal * rhs_x + rotation * rhs_y) * inverse
            y = (diagonal * rhs_y - rotation * rhs_x) * inverse
            vel[j, 0] = x
            vel[j, 1] = y
            if not final:
                return pack_velocity(j, cols, x, y)
            slip_x, slip_y = cur_x - x, cur_y - y
            drag = jnp.sqrt(slip_x * slip_x + slip_y * slip_y + speed_floor * speed_floor)
            area = area_buf[j]
            blend[0, j] = area * drag * slip_x + (1.0 - area) * wind_x
            blend[1, j] = area * drag * slip_y + (1.0 - area) * wind_y
            return cols

        cols = (zero, zero)
        if sweep == 0:
            for s in range(chunks):

                @pl.when(me != s)
                def _():
                    out_copy(0, s).wait_recv()
                    fwd_copy(s, lev).start()

            for s in range(chunks):

                @pl.when(me != s)
                def _():
                    fwd_copy(s, 1 - lev).wait_recv()
                    fwd_copy(s, lev).wait_send()

            for s in range(1, chunks + 1):

                @pl.when(me == edge_owner(s))
                def _():
                    edge_copy(s, me).wait_recv()
                    for j in range(SCOLS):
                        for f in range(4):
                            spot_j = s * cap - SCOLS + j
                            forcing[f // 2, spot_j, f % 2] += edge_land[s, j, f]

        if final:
            for s in range(chunks):
                lax.fori_loop(s * cap, (s + 1) * cap, flow_body, cols, unroll=UNROLL)

                @pl.when(me != s)
                def _():
                    ret_copy(s, me).start()

            for s in range(1, chunks + 1):

                @pl.when(me == edge_owner(s))
                def _():
                    ret_edge_copy(s).start()

        else:
            cols = lax.fori_loop(0, slots, flow_body, cols, unroll=UNROLL)
            put_cols(vel_sec, cols)
            halo_start(vel_halo)

    @pl.when(full)
    def _():
        def keep(j, c):
            for f in range(2):
                back[f, me * cap + j] = blend[f, me * cap + j]
            return c

        lax.fori_loop(0, cap, keep, 0, unroll=UNROLL)

    def back_copy(o, half):
        place = back.at[half, pl.ds(o * cap, cap)]
        return remote(place, place, back_send.at[o], back_recv.at[o], partner)

    @pl.when(full)
    def _():
        for delta in range(1, owners):
            o = lax.rem(me + delta, owners)
            ret_copy(0, o).wait_recv()
            back_copy(o, lev).start()
        for delta in range(1, owners):
            o = lax.rem(me + delta, owners)
            back_copy(o, 1 - lev).wait_recv()
            back_copy(o, lev).wait_send()

    @pl.when(has_edge(me))
    def _():
        ret_edge_copy(me).wait_recv()
        edge_copy(me, edge_owner(me)).wait_send()

    @pl.when(full)
    def _():
        for delta in range(1, owners):
            out_copy(lax.rem(me + delta, owners), me).wait_send()

    for s in range(chunks):

        @pl.when(me != s)
        def _():
            ret_copy(s, me).wait_send()

    for s in range(1, chunks + 1):

        @pl.when(me == edge_owner(s))
        def _():
            ret_edge_copy(s).wait_send()

    def ocean_body(b, c):
        lane = lane_ref[b]
        safe = jnp.maximum(lane, 0)
        for f in range(2):
            ocean_out[b, f] = jnp.where(lane >= 0, back[f, safe], ocean_ref[b, f])
        return c

    lax.fori_loop(0, blocks, ocean_body, 0, unroll=UNROLL)


def on_device(ocean_forcing, ice_home, ice_velocity, ice_stress, ice_area, ice_thick, neighbors):
    owners = lax.axis_size("blk")
    sectors = lax.axis_size("sub")
    me = lax.axis_index("blk")
    sector = lax.axis_index("sub")
    home = ice_home[0]
    table = neighbors[0]
    blocks = ocean_forcing.shape[1]
    slots = ice_velocity.shape[1]
    cap = blocks // owners
    chunks = slots // cap
    section = 2 * slots + 16

    present = home >= 0
    position = home % slots - me * cap
    lane = jnp.where(position >= 0, home // slots * cap + position, blocks + SCOLS + position)
    lane = jnp.where(present, lane, -1)
    wanted = jnp.arange(blocks + SCOLS, dtype=jnp.int32)
    ids = jnp.arange(blocks, dtype=jnp.int32)
    src = jnp.max(jnp.where(wanted[:, None] == lane[None, :], ids[None, :], -1), axis=1)

    beside = table.T
    rows = jnp.stack([beside[0], beside[2]])
    across = rows // slots // sectors - me + 1
    rows_at = jnp.where(rows >= 0, jnp.clip(across, 0, 2) * section + rows % slots, 3 * section)
    beside = jnp.pad(beside, ((0, 2), (0, 128 - slots)), constant_values=-1)

    f32 = jnp.float32
    tile = ocean_forcing.shape[3:]
    vmem = pl.BlockSpec(memory_space=pltpu.VMEM)
    smem = pl.BlockSpec(memory_space=pltpu.SMEM)
    dma = pltpu.SemaphoreType.DMA
    outs = pl.pallas_call(
        functools.partial(kernel, owners, sectors),
        out_shape=(
            jax.ShapeDtypeStruct((blocks, 2) + tile, f32),
            jax.ShapeDtypeStruct((slots, 2) + tile, f32),
            jax.ShapeDtypeStruct((slots, 3) + tile, f32),
        ),
        in_specs=[smem] * 3 + [vmem] * 6,
        out_specs=(vmem,) * 3,
        scratch_shapes=[
            pltpu.VMEM((owners, cap, 2) + tile, f32),
            pltpu.VMEM((SCOLS, 4) + tile, f32),
            pltpu.VMEM((2, slots, 2) + tile, f32),
            pltpu.VMEM((chunks + 1, SCOLS, 4) + tile, f32),
            pltpu.VMEM((2, 2, slots) + tile, f32),
            pltpu.VMEM((slots,) + tile, f32),
            pltpu.VMEM((slots,) + tile, f32),
            pltpu.VMEM((slots,) + tile, f32),
            pltpu.VMEM((2, slots) + tile, f32),
            pltpu.VMEM((2, blocks + SCOLS) + tile, f32),
            pltpu.VMEM((4 * section, 128), f32),
            pltpu.VMEM((3, 16, 128), f32),
            pltpu.VMEM((4 * section, 128), f32),
            pltpu.VMEM((3, 16, 128), f32),
            pltpu.VMEM((6 * 128, 128), jnp.bfloat16),
            pltpu.VMEM((6 * 128, 128), jnp.bfloat16),
            dma((owners,)),
            dma((owners,)),
            dma((chunks + 2,)),
            dma((chunks,)),
            dma((chunks,)),
            dma((2,)),
            dma((10,)),
            dma((10,)),
            dma((chunks,)),
            dma((owners,)),
            dma((chunks + 2,)),
            dma((owners,)),
            dma((owners,)),
        ],
        compiler_params=pltpu.CompilerParams(
            collective_id=0, has_side_effects=True, vmem_limit_bytes=48 * 2**20
        ),
    )(
        src,
        lane,
        rows_at.reshape(2 * slots),
        beside,
        ocean_forcing[0],
        ice_velocity[0],
        ice_stress[0],
        ice_area[0],
        ice_thick[0],
    )
    return tuple(out[None] for out in outs)


def solution(mesh):
    return jax.shard_map(
        on_device,
        mesh=mesh,
        in_specs=(
            P(("groups", "sub"), "blk", None, None, None),
            P(("groups", "sub"), "blk"),
            P(("groups", "sub"), "blk", None, None, None),
            P(("groups", "sub"), "blk", None, None, None),
            P(("groups", "sub"), "blk", "lev", None, None),
            P(("groups", "sub"), "blk", "lev", None, None),
            P(("groups", "sub"), "blk", None),
        ),
        out_specs=(
            P(("groups", "sub"), "blk", None, None, None),
            P(("groups", "sub"), "blk", None, None, None),
            P(("groups", "sub"), "blk", None, None, None),
        ),
        check_vma=False,
    )
```

```python
import functools
import types

import jax
import jax.numpy as jnp
from jax import lax
from jax.experimental import pallas as pl
from jax.experimental.pallas import tpu as pltpu
from jax.sharding import PartitionSpec as P

SCOLS = 4
ITERS = 4
VMEM_MB = 56

strength_scale = 4.0
cover_decay = 4.0
elastic_weight = 1.0
ellipse_square = 4.0
delta_floor = 0.05
inertia = 2.0
speed_floor = 0.2
coriolis = 0.6

MESH = pl.DeviceIdType.MESH


SCRATCH = (
    "ocean_ref", "vel", "sig", "area_in", "thick_in", "ocean_acc", "send_buf", "edge_send",
    "forcing", "edge_land", "cover", "area_buf", "mass_buf", "strength_buf", "blend", "back",
    "rows_0", "rows_1", "rows_i", "next_0", "next_1", "prev_0", "prev_1", "prev_i", "pick_next",
    "pick_prev", "first_rows", "ghost_flow", "ghost_row", "ghost_col", "upper", "corner",
    "local_sems", "out_send", "out_recv", "edge_sems", "fwd_send", "fwd_recv", "cover_sems",
    "halo_send", "halo_recv", "ret_send", "ret_recv", "ret_edge", "back_send", "back_recv",
)


def stress_update(flow_x, flow_y, down_x, down_y, right_x, right_y, one, two, shear, strength):
    stretch_x = down_x - flow_x
    stretch_y = right_y - flow_y
    shear_rate = right_x - flow_x + (down_y - flow_y)
    divergence = stretch_x + stretch_y
    tension = stretch_x - stretch_y
    square = (
        divergence * divergence
        + (tension * tension + shear_rate * shear_rate) * (1.0 / ellipse_square)
        + delta_floor * delta_floor
    )
    weight = elastic_weight * strength * lax.rsqrt(square)
    relax = 1.0 / (1.0 + elastic_weight)
    return (
        (one + weight * divergence - elastic_weight * strength) * relax,
        (two + weight * tension * (1.0 / ellipse_square)) * relax,
        (shear + weight * shear_rate * (0.5 / ellipse_square)) * relax,
    )


def kernel(owners, sectors, *refs):
    (
        src_ref,
        lane_ref,
        row_ref,
        beside_ref,
        ocean_hbm,
        vel_hbm,
        stress_hbm,
        area_hbm,
        thick_hbm,
        ocean_out,
        vel_out,
        sig_out,
    ) = refs[:12]
    r = types.SimpleNamespace(**dict(zip(SCRATCH, refs[12:], strict=True)))
    group = lax.axis_index("groups")
    me = lax.axis_index("blk")
    sector = lax.axis_index("sub")
    lev = lax.axis_index("lev")
    ocean_ref, vel, sig, forcing, blend, back = (
        r.ocean_ref, r.vel, r.sig, r.forcing, r.blend, r.back
    )
    slots = vel.shape[0]
    blocks = ocean_ref.shape[0]
    cap = blocks // owners
    chunks = slots // cap
    half = slots // 2
    unit = 4 * half + 32
    f32 = jnp.float32

    def at(blk, sub=None, core=None):
        return (
            group,
            blk,
            sector if sub is None else sub,
            lev if core is None else core,
        )

    partner = at(me, None, 1 - lev)

    def remote(src, dst, send, recv, target):
        return pltpu.make_async_remote_copy(
            src_ref=src,
            dst_ref=dst,
            send_sem=send,
            recv_sem=recv,
            device_id=target,
            device_id_type=MESH,
        )

    local = [
        pltpu.make_async_copy(src, dst, r.local_sems.at[i])
        for i, (src, dst) in enumerate((
            (ocean_hbm, ocean_ref),
            (vel_hbm, vel),
            (area_hbm, r.area_in),
            (thick_hbm, r.thick_in),
            (stress_hbm, sig),
        ))
    ]
    for copy in local:
        copy.start()

    lanes = lax.broadcasted_iota(jnp.int32, (8, 128), 1)
    subs = lax.broadcasted_iota(jnp.int32, (8, 128), 0)
    zero = jnp.zeros((8, 128), f32)

    rows = (r.rows_0, r.rows_1)
    crossed_next = (r.next_0, r.next_1)
    crossed_prev = (r.prev_0, r.prev_1)
    for ref in (*rows, r.rows_i):
        for a in (2, 3):
            ref[a * unit + 4 * half : (a + 1) * unit, :] = jnp.zeros((32, 128), f32)
        rest = ref.shape[0] - 4 * unit
        ref[4 * unit :, :] = jnp.zeros((rest, 128), f32)
    for ref in (*crossed_next, *crossed_prev, r.prev_i):
        ref[...] = jnp.zeros(ref.shape, f32)

    barrier = pltpu.get_barrier_semaphore()

    def greet(target):
        pl.semaphore_signal(barrier, inc=1, device_id=target, device_id_type=MESH)

    greet(partner)
    for delta in range(1, owners):
        greet(at(lax.rem(me + delta, owners)))
    expected = owners
    for ds in (-1, 1):
        for da in (-1, 0, 1):
            q, o = sector + ds, me + da
            ok = (q >= 0) & (q < sectors) & (o >= 0) & (o < owners)

            @pl.when(ok)
            def _():
                greet(at(o, q))

            expected = expected + ok.astype(jnp.int32)
    local[0].wait()
    pl.semaphore_wait(barrier, expected)

    def out_copy(o, s):
        return remote(
            r.send_buf.at[o],
            forcing.at[lev, pl.ds(s * cap, cap)],
            r.out_send.at[o],
            r.out_recv.at[s],
            at(o),
        )

    full = me * cap < slots

    def take(lane, fields):
        src = src_ref[lane]
        safe = jnp.maximum(src, 0)
        return [jnp.where(src >= 0, ocean_ref[safe, f], 0.0) for f in fields]

    for delta in range(1, owners):
        o = lax.rem(me + delta, owners)

        @pl.when(full)
        def _():
            def fill(g, c):
                tiles = [take(o * cap + 4 * g + i, (2 * lev, 2 * lev + 1)) for i in range(4)]
                for i in range(4):
                    for f in range(2):
                        r.send_buf[o, 4 * g + i, f] = tiles[i][f]
                return c

            lax.fori_loop(0, cap // 4, fill, 0)
            out_copy(o, me).start()

    def edge_owner(s):
        last_pass = s * (cap // SCOLS) - 1
        return jnp.where(lax.rem(last_pass + 2, 2) == 0, owners - 1, 0)

    def has_edge(s):
        return (s >= 1) & (s <= chunks)

    def edge_copy(s, o):
        return remote(
            r.edge_send, r.edge_land.at[s], r.edge_sems.at[0], r.edge_sems.at[1 + s], at(o)
        )

    @pl.when(has_edge(me))
    def _():
        for j in range(SCOLS):
            tiles = take(blocks + j, range(4))
            for f in range(4):
                r.edge_send[j, f] = tiles[f]
        edge_copy(me, edge_owner(me)).start()

    def line_copies(ref, base):
        return [
            (me + 1 < owners, remote(
                ref.at[pl.ds(0, unit)], ref.at[pl.ds(2 * unit, unit)],
                r.halo_send.at[base], r.halo_recv.at[base], at(me + 1)), me >= 1),
            (me >= 1, remote(
                ref.at[pl.ds(unit, unit)], ref.at[pl.ds(3 * unit, unit)],
                r.halo_send.at[base + 1], r.halo_recv.at[base + 1], at(me - 1)),
                me + 1 < owners),
        ]

    def cross_copies(cols, cross, down, base):
        target, source = sector + down, sector - down
        t_ok = (target >= 0) & (target < sectors)
        s_ok = (source >= 0) & (source < sectors)
        made = []
        for i, da in enumerate((1, 0, -1)):
            o, p = me + da, me - da
            made.append((t_ok & (o >= 0) & (o < owners), remote(
                cols, cross.at[1 - da], r.halo_send.at[base + i], r.halo_recv.at[base + i],
                at(o, target)), s_ok & (p >= 0) & (p < owners)))
        return made

    def halo_copies(parity):
        ref, base = rows[parity], 8 * parity
        first = ref.at[pl.ds(4 * half, 16)]
        last = ref.at[pl.ds(4 * half + 16, 16)]
        return (
            cross_copies(first, crossed_next[parity], -1, base + 2)
            + cross_copies(last, crossed_prev[parity], 1, base + 5)
            + line_copies(ref, base)
        )

    halos = [halo_copies(0), halo_copies(1)]
    start_halo = cross_copies(
        r.rows_i.at[pl.ds(4 * half, 32)], r.prev_i, 1, 18
    ) + line_copies(r.rows_i, 16)

    def halo_start(copies):
        for ok, copy, _ in copies:
            pl.when(ok)(copy.start)

    def halo_wait(copies):
        for ok, copy, arriving in copies:
            pl.when(arriving)(copy.wait_recv)
            pl.when(ok)(copy.wait_send)

    def put_cols(ref, cols):
        for i, col in enumerate(cols):
            for a in range(2):
                low = a * unit + 4 * half + 8 * i
                ref[low : low + 8, :] = col

    def pack_flow(ref, g, flows, cols):
        cols = list(cols)
        for i, (x, y) in enumerate(flows):
            odd, pos = i // 4, 4 * g + i % 4
            first = 2 * half if odd else unit
            last = unit + 2 * half if odd else 0
            for f, tile in enumerate((x, y)):
                ref[pl.ds(first + f * half + pos, 1), :] = tile[0:1]
                ref[pl.ds(last + f * half + pos, 1), :] = tile[7:8]
                r.first_rows[f, pl.ds(8 * g + i, 1), :] = tile[0:1]
            here = lanes == 8 * g + i
            for f, tile in enumerate((x, y)):
                cols[f] = jnp.where(here, tile[:, 0:1], cols[f])
                cols[2 + f] = jnp.where(here, tile[:, 127:128], cols[2 + f])
        return tuple(cols)

    def start_body(g, cols):
        flows = [(vel[8 * g + i, 0], vel[8 * g + i, 1]) for i in range(8)]
        return pack_flow(rows[0], g, flows, cols)

    local[1].wait()
    cols = lax.fori_loop(0, slots // 8, start_body, (zero,) * 4)
    put_cols(rows[0], cols)
    halo_start(halos[0])

    local[2].wait()
    local[3].wait()

    def part_body(g, c):
        made = []
        for i in range(4):
            j = 4 * g + i
            first, second = r.area_in[j, 0], r.area_in[j, 1]
            made.append((
                first + second,
                first * r.thick_in[j, 0] + second * r.thick_in[j, 1],
            ))
        for i in range(4):
            r.cover[0, 0, 4 * g + i] = made[i][0]
            r.cover[0, 1, 4 * g + i] = made[i][1]
        return c

    lax.fori_loop(0, slots // 4, part_body, 0)
    cover_copy = remote(
        r.cover.at[0], r.cover.at[1], r.cover_sems.at[0], r.cover_sems.at[1], partner
    )
    cover_copy.start()

    @pl.when(full)
    def _():
        def fill(g, c):
            tiles = [take(me * cap + 2 * g + i, range(4)) for i in range(2)]
            for i in range(2):
                for f in range(4):
                    forcing[f // 2, me * cap + 2 * g + i, f % 2] = tiles[i][f]
            return c

        lax.fori_loop(0, cap // 2, fill, 0)

    spot = lax.broadcasted_iota(jnp.int32, (128, 128), 0)
    for pick, d, toward, low in (
        (r.pick_next, 1, 1, 0),
        (r.pick_next, 4, 1, 128),
        (r.pick_prev, 3, -1, 0),
        (r.pick_prev, 5, -1, 128),
    ):
        ids = beside_ref[d : d + 1, :]
        for i in range(6):
            across, aside = i % 3 - 1, (i // 3) * toward
            base = ((me + across) * sectors + sector + aside) * slots
            hit = (ids - base == spot) & (spot < slots) & (ids >= 0)
            pick[i * 128 : (i + 1) * 128, low : low + 128] = hit.astype(f32).astype(jnp.bfloat16)

    def fetch_columns(ref, low, count, cross, pick):
        parts = [
            ref[a * unit + 4 * half + low : a * unit + 4 * half + low + count, :]
            for a in (2, 0, 3)
        ] + [cross[a] for a in range(3)]
        whole = jnp.concatenate(parts, axis=1)
        first = whole.astype(jnp.bfloat16)
        rest = whole - first.astype(f32)
        second = rest.astype(jnp.bfloat16)
        third = (rest - second.astype(f32)).astype(jnp.bfloat16)
        terms = jnp.concatenate([first, second, third], axis=0)
        got = jnp.dot(terms, pick[...], preferred_element_type=f32)
        return got[0:count] + got[count : 2 * count] + got[2 * count : 3 * count]

    local[4].wait()
    cover_copy.wait()

    def cover_body(g, cols):
        cols = list(cols)
        for part in range(2):
            made = []
            for i in range(4):
                j = 8 * g + 4 * part + i
                area = r.cover[0, 0, j] + r.cover[1, 0, j]
                volume = r.cover[0, 1, j] + r.cover[1, 1, j]
                strength = strength_scale * volume * jnp.exp(-cover_decay * (1.0 - area))
                made.append((area, volume, strength, [sig[j, f] for f in range(3)] + [strength]))
            for i, (area, volume, strength, fields) in enumerate(made):
                j = 8 * g + 4 * part + i
                r.area_buf[j] = area
                r.mass_buf[j] = volume
                r.strength_buf[j] = strength
                for f, tile in enumerate(fields):
                    r.rows_i[pl.ds(part * unit + f * half + 4 * g + i, 1), :] = tile[7:8]
                    cols[f] = jnp.where(lanes == j, tile[:, 127:128], cols[f])
        return tuple(cols)

    cols = lax.fori_loop(0, slots // 8, cover_body, (zero,) * 4)
    put_cols(r.rows_i, cols)
    halo_start(start_halo)

    def fwd_copy(s, part):
        place = forcing.at[part, pl.ds(s * cap, cap)]
        return remote(place, place, r.fwd_send.at[s], r.fwd_recv.at[s], partner)

    def ret_copy(s, o):
        return remote(
            blend.at[lev, pl.ds(s * cap, cap)],
            back.at[lev, pl.ds(o * cap, cap)],
            r.ret_send.at[s],
            r.ret_recv.at[o],
            at(s),
        )

    def ret_edge_copy(s):
        return remote(
            blend.at[:, pl.ds(s * cap - SCOLS, SCOLS)],
            back.at[:, pl.ds(blocks, SCOLS)],
            r.ret_edge.at[1 + s],
            r.ret_edge.at[0],
            at(s),
        )

    sig_copy = pltpu.make_async_copy(sig, sig_out, r.local_sems.at[4])
    vel_copy = pltpu.make_async_copy(vel, vel_out, r.local_sems.at[1])

    for sweep in range(ITERS):
        parity = sweep % 2
        ref = rows[parity]
        final = sweep == ITERS - 1
        halo_wait(halos[parity])
        got = fetch_columns(ref, 0, 16, crossed_next[parity], r.pick_next)
        right_x, right_y = got[0:8, 0:128], got[8:16, 0:128]
        r.corner[...] = jnp.transpose(
            jnp.concatenate([got[:, 128:256], jnp.zeros((112, 128), f32)], axis=0)
        )
        got = fetch_columns(ref, 16, 16, crossed_prev[parity], r.pick_prev)
        left_x, left_y = got[0:8, 0:128], got[8:16, 0:128]
        under_x, under_y = got[0:1, 128:256], got[8:9, 128:256]

        def stress_body(g, c):
            for part in range(2):
                js = [8 * g + 4 * part + i for i in range(4)]
                last_row, last_col = subs == 7, lanes == 127
                made = []
                for j in js:
                    x, y = vel[j, 0], vel[j, 1]
                    place = row_ref[j]
                    above = row_ref[slots + j]
                    below_x = ref[pl.ds(place, 1), :]
                    below_y = ref[pl.ds(place + half, 1), :]
                    above_x = ref[pl.ds(above, 1), :]
                    above_y = ref[pl.ds(above + half, 1), :]
                    turn = 127 - j
                    new = stress_update(
                        x,
                        y,
                        jnp.where(last_row, below_x, pltpu.roll(x, 7, 0)),
                        jnp.where(last_row, below_y, pltpu.roll(y, 7, 0)),
                        jnp.where(last_col, pltpu.roll(right_x, turn, 1), pltpu.roll(x, 127, 1)),
                        jnp.where(last_col, pltpu.roll(right_y, turn, 1), pltpu.roll(y, 127, 1)),
                        sig[j, 0],
                        sig[j, 1],
                        sig[j, 2],
                        r.strength_buf[j],
                    )
                    made.append((new, above_x, above_y))
                for j, (new, above_x, above_y) in zip(js, made):
                    for f in range(3):
                        sig[j, f] = new[f]
                    r.ghost_flow[0, pl.ds(j, 1), :] = above_x
                    r.ghost_flow[1, pl.ds(j, 1), :] = above_y
            return c

        lax.fori_loop(0, slots // 8, stress_body, 0)
        if final:
            sig_copy.start()

        if sweep == 0:
            halo_wait(start_halo)

            def gather_body(g, c):
                for i in range(8):
                    j = 8 * g + i
                    place = row_ref[2 * slots + j]
                    for f in range(4):
                        r.ghost_row[f, pl.ds(j, 1), :] = r.rows_i[pl.ds(place + f * half, 1), :]
                return c

            lax.fori_loop(0, slots // 8, gather_body, 0)
            got = fetch_columns(r.rows_i, 0, 32, r.prev_i, r.pick_prev)
            for f in range(4):
                r.ghost_col[f] = got[8 * f : 8 * f + 8, 0:128]

        own_first = [
            ref[4 * half + 8 * f : 4 * half + 8 * f + 8, :] for f in range(2)
        ]
        new = stress_update(
            left_x,
            left_y,
            jnp.where(subs == 7, under_x, pltpu.roll(left_x, 7, 0)),
            jnp.where(subs == 7, under_y, pltpu.roll(left_y, 7, 0)),
            own_first[0],
            own_first[1],
            *[r.ghost_col[f] for f in range(4)],
        )
        for f in range(3):
            r.ghost_col[f] = new[f]
        left_shear = new[2]
        left_normal = 0.5 * (new[0] - new[1])

        def ghost_body(g, c):
            made = []
            for i in range(2):
                here = pl.ds(pl.multiple_of(16 * g + 8 * i, 8), 8)
                x, y = r.ghost_flow[0, here, :], r.ghost_flow[1, here, :]
                end = r.corner[here, :]
                new = stress_update(
                    x,
                    y,
                    r.first_rows[0, here, :],
                    r.first_rows[1, here, :],
                    jnp.where(lanes == 127, end[:, 7:8], pltpu.roll(x, 127, 1)),
                    jnp.where(lanes == 127, end[:, 15:16], pltpu.roll(y, 127, 1)),
                    *[r.ghost_row[f, here, :] for f in range(4)],
                )
                made.append((here, new))
            for here, new in made:
                for f in range(3):
                    r.ghost_row[f, here, :] = new[f]
                r.upper[0, here, :] = 0.5 * (new[0] + new[1])
                r.upper[1, here, :] = new[2]
            return c

        lax.fori_loop(0, slots // 16, ghost_body, 0)

        if sweep == 0:
            for s in range(chunks):

                @pl.when(me != s)
                def _():
                    out_copy(0, s).wait_recv()
                    fwd_copy(s, lev).start()

            for s in range(chunks):

                @pl.when(me != s)
                def _():
                    fwd_copy(s, 1 - lev).wait_recv()
                    fwd_copy(s, lev).wait_send()

            for s in range(1, chunks + 1):

                @pl.when(me == edge_owner(s))
                def _():
                    edge_copy(s, me).wait_recv()
                    for j in range(SCOLS):
                        for f in range(4):
                            spot_j = s * cap - SCOLS + j
                            forcing[f // 2, spot_j, f % 2] += r.edge_land[s, j, f]

        def flow_body(g, cols):
            here = pl.ds(pl.multiple_of(8 * g, 8), 8)
            upper_n, upper_s = r.upper[0, here, :], r.upper[1, here, :]
            flows = []
            first_row, first_col = subs == 0, lanes == 0
            for part in range(2):
                js = [8 * g + 4 * part + i for i in range(4)]
                made = []
                for i, j in enumerate(js):
                    k = 4 * part + i
                    x, y = vel[j, 0], vel[j, 1]
                    one, two, shear = sig[j, 0], sig[j, 1], sig[j, 2]
                    normal_x = 0.5 * (one + two)
                    normal_y = 0.5 * (one - two)
                    turn = jnp.where(j == 0, 0, 128 - j)
                    above_normal = jnp.where(
                        first_row, upper_n[k : k + 1], pltpu.roll(normal_x, 1, 0)
                    )
                    above_shear = jnp.where(
                        first_row, upper_s[k : k + 1], pltpu.roll(shear, 1, 0)
                    )
                    before_shear = jnp.where(
                        first_col, pltpu.roll(left_shear, turn, 1), pltpu.roll(shear, 1, 1)
                    )
                    before_normal = jnp.where(
                        first_col, pltpu.roll(left_normal, turn, 1), pltpu.roll(normal_y, 1, 1)
                    )
                    force_x = normal_x - above_normal + (shear - before_shear)
                    force_y = shear - above_shear + (normal_y - before_normal)
                    wind_x, wind_y = forcing[0, j, 0], forcing[0, j, 1]
                    cur_x, cur_y = forcing[1, j, 0], forcing[1, j, 1]
                    slip_x, slip_y = cur_x - x, cur_y - y
                    drag = jnp.sqrt(slip_x * slip_x + slip_y * slip_y + speed_floor * speed_floor)
                    mass = r.mass_buf[j]
                    heavy = mass * inertia
                    diagonal = heavy + drag
                    rotation = mass * coriolis
                    rhs_x = heavy * x + force_x + wind_x + drag * cur_x
                    rhs_y = heavy * y + force_y + wind_y + drag * cur_y
                    inverse = 1.0 / (diagonal * diagonal + rotation * rotation)
                    x = (diagonal * rhs_x + rotation * rhs_y) * inverse
                    y = (diagonal * rhs_y - rotation * rhs_x) * inverse
                    share = None
                    if final:
                        slip_x, slip_y = cur_x - x, cur_y - y
                        drag = jnp.sqrt(
                            slip_x * slip_x + slip_y * slip_y + speed_floor * speed_floor
                        )
                        area = r.area_buf[j]
                        share = (
                            area * drag * slip_x + (1.0 - area) * wind_x,
                            area * drag * slip_y + (1.0 - area) * wind_y,
                        )
                    made.append((x, y, share))
                for j, (x, y, share) in zip(js, made):
                    vel[j, 0] = x
                    vel[j, 1] = y
                    flows.append((x, y))
                    if final:
                        blend[0, j] = share[0]
                        blend[1, j] = share[1]
            if final:
                return cols
            return pack_flow(rows[1 - parity], g, flows, cols)

        if final:
            step = max(cap, 8)
            for low in range(0, slots, step):
                lax.fori_loop(low // 8, (low + step) // 8, flow_body, 0)
                for s in range(low // cap, (low + step) // cap):

                    @pl.when(me != s)
                    def _():
                        ret_copy(s, me).start()

            for s in range(1, chunks + 1):

                @pl.when(me == edge_owner(s))
                def _():
                    ret_edge_copy(s).start()

            vel_copy.start()
        else:
            cols = lax.fori_loop(0, slots // 8, flow_body, (zero,) * 4)
            put_cols(rows[1 - parity], cols)
            halo_start(halos[1 - parity])

    @pl.when(full)
    def _():
        def keep(g, c):
            tiles = [[blend[f, me * cap + 4 * g + i] for f in range(2)] for i in range(4)]
            for i in range(4):
                for f in range(2):
                    back[f, me * cap + 4 * g + i] = tiles[i][f]
            return c

        lax.fori_loop(0, cap // 4, keep, 0)

    def back_copy(o, part):
        place = back.at[part, pl.ds(o * cap, cap)]
        return remote(place, place, r.back_send.at[o], r.back_recv.at[o], partner)

    @pl.when(full)
    def _():
        for delta in range(1, owners):
            o = lax.rem(me + delta, owners)
            ret_copy(0, o).wait_recv()
            back_copy(o, lev).start()
        for delta in range(1, owners):
            o = lax.rem(me + delta, owners)
            back_copy(o, 1 - lev).wait_recv()
            back_copy(o, lev).wait_send()

    @pl.when(has_edge(me))
    def _():
        ret_edge_copy(me).wait_recv()
        edge_copy(me, edge_owner(me)).wait_send()

    def ocean_body(g, c):
        made = []
        for i in range(4):
            b = 4 * g + i
            lane = lane_ref[b]
            safe = jnp.maximum(lane, 0)
            made.append([
                jnp.where(lane >= 0, back[f, safe], ocean_ref[b, f]) for f in range(2)
            ])
        for i in range(4):
            for f in range(2):
                r.ocean_acc[4 * g + i, f] = made[i][f]
        return c

    lax.fori_loop(0, blocks // 4, ocean_body, 0)
    ocean_copy = pltpu.make_async_copy(r.ocean_acc, ocean_out, r.local_sems.at[0])
    ocean_copy.start()

    @pl.when(full)
    def _():
        for delta in range(1, owners):
            out_copy(lax.rem(me + delta, owners), me).wait_send()

    for s in range(chunks):

        @pl.when(me != s)
        def _():
            ret_copy(s, me).wait_send()

    for s in range(1, chunks + 1):

        @pl.when(me == edge_owner(s))
        def _():
            ret_edge_copy(s).wait_send()

    sig_copy.wait()
    vel_copy.wait()
    ocean_copy.wait()


def on_device(ocean_forcing, ice_home, ice_velocity, ice_stress, ice_area, ice_thick, neighbors):
    owners = lax.axis_size("blk")
    sectors = lax.axis_size("sub")
    me = lax.axis_index("blk")
    home = ice_home[0]
    blocks = ocean_forcing.shape[1]
    slots = ice_velocity.shape[1]
    cap = blocks // owners
    chunks = slots // cap
    half = slots // 2
    unit = 4 * half + 32

    position = lax.rem(home, slots) - me * cap
    lane = jnp.where(
        position >= 0, lax.div(home, slots) * cap + position, blocks + SCOLS + position
    )
    lane = jnp.where(home >= 0, lane, -1)
    wanted = jnp.arange(blocks + SCOLS, dtype=jnp.int32)
    ids = jnp.arange(blocks, dtype=jnp.int32)
    src = jnp.max(jnp.where(wanted[:, None] == lane[None, :], ids[None, :], -1), axis=1)

    beside = neighbors[0].T

    def places(ids, own_even, own_odd, prev, following):
        across = lax.div(ids, slots * sectors) - me
        slot = lax.rem(ids, slots)
        turn = lax.div(slot, SCOLS)
        pos = lax.div(turn, 2) * SCOLS + lax.rem(slot, SCOLS)
        own = jnp.where(lax.rem(turn, 2) == 1, own_odd, own_even)
        start = jnp.where(across == 0, own, jnp.where(across < 0, prev, following))
        return jnp.where(ids >= 0, jnp.clip(start + pos, 0, 4 * unit), 4 * unit)

    rows_at = jnp.concatenate([
        places(beside[0], unit, 2 * half, 2 * unit + 2 * half, 3 * unit),
        places(beside[2], 0, unit + 2 * half, 2 * unit, 3 * unit + 2 * half),
        places(beside[2], 0, unit, 2 * unit, 3 * unit),
    ])
    beside = jnp.pad(beside, ((0, 2), (0, 128 - slots)), constant_values=-1)

    f32 = jnp.float32
    tile = ocean_forcing.shape[3:]
    vmem = pl.BlockSpec(memory_space=pltpu.VMEM)
    smem = pl.BlockSpec(memory_space=pltpu.SMEM)
    anywhere = pl.BlockSpec(memory_space=pl.ANY)
    dma = pltpu.SemaphoreType.DMA

    def tiles(*lead):
        return pltpu.VMEM(lead + tile, f32)

    lines = 4 * unit + 3 * half + 8
    scratch = dict(
        ocean_ref=tiles(blocks, 4),
        vel=tiles(slots, 2),
        sig=tiles(slots, 3),
        area_in=tiles(slots, 2),
        thick_in=tiles(slots, 2),
        ocean_acc=tiles(blocks, 2),
        send_buf=tiles(owners, cap, 2),
        edge_send=tiles(SCOLS, 4),
        forcing=tiles(2, slots, 2),
        edge_land=tiles(chunks + 1, SCOLS, 4),
        cover=tiles(2, 2, slots),
        area_buf=tiles(slots),
        mass_buf=tiles(slots),
        strength_buf=tiles(slots),
        blend=tiles(2, slots),
        back=tiles(2, blocks + SCOLS),
        rows_0=pltpu.VMEM((lines, 128), f32),
        rows_1=pltpu.VMEM((lines, 128), f32),
        rows_i=pltpu.VMEM((lines, 128), f32),
        next_0=pltpu.VMEM((3, 16, 128), f32),
        next_1=pltpu.VMEM((3, 16, 128), f32),
        prev_0=pltpu.VMEM((3, 16, 128), f32),
        prev_1=pltpu.VMEM((3, 16, 128), f32),
        prev_i=pltpu.VMEM((3, 32, 128), f32),
        pick_next=pltpu.VMEM((6 * 128, 256), jnp.bfloat16),
        pick_prev=pltpu.VMEM((6 * 128, 256), jnp.bfloat16),
        first_rows=pltpu.VMEM((2, slots, 128), f32),
        ghost_flow=pltpu.VMEM((2, slots, 128), f32),
        ghost_row=pltpu.VMEM((4, slots, 128), f32),
        ghost_col=tiles(4),
        upper=pltpu.VMEM((2, slots, 128), f32),
        corner=pltpu.VMEM((128, 128), f32),
        local_sems=dma((5,)),
        out_send=dma((owners,)),
        out_recv=dma((owners,)),
        edge_sems=dma((chunks + 2,)),
        fwd_send=dma((chunks,)),
        fwd_recv=dma((chunks,)),
        cover_sems=dma((2,)),
        halo_send=dma((21,)),
        halo_recv=dma((21,)),
        ret_send=dma((chunks,)),
        ret_recv=dma((owners,)),
        ret_edge=dma((chunks + 2,)),
        back_send=dma((owners,)),
        back_recv=dma((owners,)),
    )
    outs = pl.pallas_call(
        functools.partial(kernel, owners, sectors),
        out_shape=(
            jax.ShapeDtypeStruct((blocks, 2) + tile, f32),
            jax.ShapeDtypeStruct((slots, 2) + tile, f32),
            jax.ShapeDtypeStruct((slots, 3) + tile, f32),
        ),
        in_specs=[smem] * 3 + [vmem] + [anywhere] * 5,
        out_specs=(anywhere,) * 3,
        scratch_shapes=[scratch[name] for name in SCRATCH],
        compiler_params=pltpu.CompilerParams(
            collective_id=0, has_side_effects=True, vmem_limit_bytes=VMEM_MB * 2**20
        ),
    )(
        src,
        lane,
        rows_at,
        beside,
        ocean_forcing[0],
        ice_velocity[0],
        ice_stress[0],
        ice_area[0],
        ice_thick[0],
    )
    return tuple(out[None] for out in outs)


def solution(mesh):
    return jax.shard_map(
        on_device,
        mesh=mesh,
        in_specs=(
            P(("groups", "sub"), "blk", None, None, None),
            P(("groups", "sub"), "blk"),
            P(("groups", "sub"), "blk", None, None, None),
            P(("groups", "sub"), "blk", None, None, None),
            P(("groups", "sub"), "blk", "lev", None, None),
            P(("groups", "sub"), "blk", "lev", None, None),
            P(("groups", "sub"), "blk", None),
        ),
        out_specs=(
            P(("groups", "sub"), "blk", None, None, None),
            P(("groups", "sub"), "blk", None, None, None),
            P(("groups", "sub"), "blk", None, None, None),
        ),
        check_vma=False,
    )
```

```python
import functools
import types

import jax
import jax.numpy as jnp
from jax import lax
from jax.experimental import pallas as pl
from jax.experimental.pallas import tpu as pltpu
from jax.sharding import PartitionSpec as P

SCOLS = 4
ITERS = 4
VMEM_MB = 56

strength_scale = 4.0
cover_decay = 4.0
elastic_weight = 1.0
ellipse_square = 4.0
delta_floor = 0.05
inertia = 2.0
speed_floor = 0.2
coriolis = 0.6

MESH = pl.DeviceIdType.MESH


SCRATCH = (
    "ocean_ref", "vel", "sig", "area_in", "thick_in", "ocean_acc", "send_buf", "edge_send",
    "forcing", "edge_land", "cover", "area_buf", "mass_buf", "strength_buf", "blend", "back",
    "rows_0", "rows_1", "rows_i", "next_0", "next_1", "prev_0", "prev_1", "prev_i", "pick_next",
    "pick_prev", "first_rows", "ghost_flow", "ghost_row", "ghost_col", "upper", "corner",
    "local_sems", "out_send", "out_recv", "edge_sems", "fwd_send", "fwd_recv", "cover_sems",
    "halo_send", "halo_recv", "ret_send", "ret_recv", "ret_edge", "back_send", "back_recv",
)


def stress_update(flow_x, flow_y, down_x, down_y, right_x, right_y, one, two, shear, strength):
    stretch_x = down_x - flow_x
    stretch_y = right_y - flow_y
    shear_rate = right_x - flow_x + (down_y - flow_y)
    divergence = stretch_x + stretch_y
    tension = stretch_x - stretch_y
    square = (
        divergence * divergence
        + (tension * tension + shear_rate * shear_rate) * (1.0 / ellipse_square)
        + delta_floor * delta_floor
    )
    weight = elastic_weight * strength * lax.rsqrt(square)
    relax = 1.0 / (1.0 + elastic_weight)
    return (
        (one + weight * divergence - elastic_weight * strength) * relax,
        (two + weight * tension * (1.0 / ellipse_square)) * relax,
        (shear + weight * shear_rate * (0.5 / ellipse_square)) * relax,
    )


def kernel(owners, sectors, *refs):
    (
        src_ref,
        lane_ref,
        row_ref,
        beside_ref,
        ocean_hbm,
        vel_hbm,
        stress_hbm,
        area_hbm,
        thick_hbm,
        ocean_out,
        vel_out,
        sig_out,
    ) = refs[:12]
    r = types.SimpleNamespace(**dict(zip(SCRATCH, refs[12:], strict=True)))
    group = lax.axis_index("groups")
    me = lax.axis_index("blk")
    sector = lax.axis_index("sub")
    lev = lax.axis_index("lev")
    ocean_ref, vel, sig, forcing, blend, back = (
        r.ocean_ref, r.vel, r.sig, r.forcing, r.blend, r.back
    )
    slots = vel.shape[0]
    blocks = ocean_ref.shape[0]
    cap = blocks // owners
    chunks = slots // cap
    half = slots // 2
    quarter = half // 2
    unit = 4 * half + 32
    f32 = jnp.float32

    def at(blk, sub=None, core=None):
        return (
            group,
            blk,
            sector if sub is None else sub,
            lev if core is None else core,
        )

    partner = at(me, None, 1 - lev)

    def remote(src, dst, send, recv, target):
        return pltpu.make_async_remote_copy(
            src_ref=src,
            dst_ref=dst,
            send_sem=send,
            recv_sem=recv,
            device_id=target,
            device_id_type=MESH,
        )

    local = [
        pltpu.make_async_copy(src, dst, r.local_sems.at[i])
        for i, (src, dst) in enumerate((
            (ocean_hbm, ocean_ref),
            (vel_hbm, vel),
            (area_hbm, r.area_in),
            (thick_hbm, r.thick_in),
            (stress_hbm, sig),
        ))
    ]
    for copy in local:
        copy.start()

    lanes = lax.broadcasted_iota(jnp.int32, (8, 128), 1)
    subs = lax.broadcasted_iota(jnp.int32, (8, 128), 0)
    zero = jnp.zeros((8, 128), f32)

    rows = (r.rows_0, r.rows_1)
    crossed_next = (r.next_0, r.next_1)
    crossed_prev = (r.prev_0, r.prev_1)
    for ref in (*rows, r.rows_i):
        for a in (2, 3):
            ref[a * unit + 4 * half : (a + 1) * unit, :] = jnp.zeros((32, 128), f32)
        rest = ref.shape[0] - 4 * unit
        ref[4 * unit :, :] = jnp.zeros((rest, 128), f32)
    for ref in (*crossed_next, *crossed_prev, r.prev_i):
        ref[...] = jnp.zeros(ref.shape, f32)

    barrier = pltpu.get_barrier_semaphore()

    def greet(target):
        pl.semaphore_signal(barrier, inc=1, device_id=target, device_id_type=MESH)

    greet(partner)
    for delta in range(1, owners):
        greet(at(lax.rem(me + delta, owners)))
    expected = owners
    for ds in (-1, 1):
        for da in (-1, 0, 1):
            q, o = sector + ds, me + da
            ok = (q >= 0) & (q < sectors) & (o >= 0) & (o < owners)

            @pl.when(ok)
            def _():
                greet(at(o, q))

            expected = expected + ok.astype(jnp.int32)
    local[0].wait()
    pl.semaphore_wait(barrier, expected)

    def out_copy(o, s):
        return remote(
            r.send_buf.at[o],
            forcing.at[lev, pl.ds(s * cap, cap)],
            r.out_send.at[o],
            r.out_recv.at[s],
            at(o),
        )

    full = me * cap < slots

    def take(lane, fields):
        src = src_ref[lane]
        safe = jnp.maximum(src, 0)
        return [jnp.where(src >= 0, ocean_ref[safe, f], 0.0) for f in fields]

    def send_share(delta):
        o = lax.rem(me + delta, owners)

        @pl.when(full)
        def _():
            def fill(g, c):
                tiles = [take(o * cap + 4 * g + i, (2 * lev, 2 * lev + 1)) for i in range(4)]
                for i in range(4):
                    for f in range(2):
                        r.send_buf[o, 4 * g + i, f] = tiles[i][f]
                return c

            lax.fori_loop(0, cap // 4, fill, 0)
            out_copy(o, me).start()

    send_share(1)

    def edge_owner(s):
        last_pass = s * (cap // SCOLS) - 1
        return jnp.where(lax.rem(last_pass + 2, 2) == 0, owners - 1, 0)

    def has_edge(s):
        return (s >= 1) & (s <= chunks)

    def edge_copy(s, o):
        return remote(
            r.edge_send, r.edge_land.at[s], r.edge_sems.at[0], r.edge_sems.at[1 + s], at(o)
        )

    @pl.when(has_edge(me))
    def _():
        for j in range(SCOLS):
            tiles = take(blocks + j, range(4))
            for f in range(4):
                r.edge_send[j, f] = tiles[f]
        edge_copy(me, edge_owner(me)).start()

    def line_copies(ref, base, low=0, high=unit):
        count = high - low
        return [
            (me + 1 < owners, remote(
                ref.at[pl.ds(low, count)], ref.at[pl.ds(2 * unit + low, count)],
                r.halo_send.at[base], r.halo_recv.at[base], at(me + 1)), me >= 1),
            (me >= 1, remote(
                ref.at[pl.ds(unit + low, count)], ref.at[pl.ds(3 * unit + low, count)],
                r.halo_send.at[base + 1], r.halo_recv.at[base + 1], at(me - 1)),
                me + 1 < owners),
        ]

    def cross_copies(cols, cross, down, base):
        target, source = sector + down, sector - down
        t_ok = (target >= 0) & (target < sectors)
        s_ok = (source >= 0) & (source < sectors)
        made = []
        for i, da in enumerate((1, 0, -1)):
            o, p = me + da, me - da
            made.append((t_ok & (o >= 0) & (o < owners), remote(
                cols, cross.at[1 - da], r.halo_send.at[base + i], r.halo_recv.at[base + i],
                at(o, target)), s_ok & (p >= 0) & (p < owners)))
        return made

    def halo_copies(parity):
        ref, base = rows[parity], 10 * parity
        first = ref.at[pl.ds(4 * half, 16)]
        last = ref.at[pl.ds(4 * half + 16, 16)]
        return (
            cross_copies(first, crossed_next[parity], -1, base + 2)
            + cross_copies(last, crossed_prev[parity], 1, base + 5)
            + line_copies(ref, base, 2 * half, unit)
        )

    def early_copies(parity):
        return line_copies(rows[parity], 10 * parity + 8, 0, 2 * half)

    early = [early_copies(0), early_copies(1)]
    halos = [halo_copies(0), halo_copies(1)]
    start_halo = cross_copies(
        r.rows_i.at[pl.ds(4 * half, 32)], r.prev_i, 1, 22
    ) + line_copies(r.rows_i, 20)

    def halo_start(copies):
        for ok, copy, _ in copies:
            pl.when(ok)(copy.start)

    def halo_wait(copies):
        for _, copy, arriving in copies:
            pl.when(arriving)(copy.wait_recv)

    def halo_sent(copies):
        for ok, copy, _ in copies:
            pl.when(ok)(copy.wait_send)

    def put_cols(ref, cols):
        for i, col in enumerate(cols):
            for a in range(2):
                low = a * unit + 4 * half + 8 * i
                ref[low : low + 8, :] = col

    def pack_flow(ref, high, g, flows, cols):
        cols = list(cols)
        for i, (x, y) in enumerate(flows):
            odd, pos = i // 4, 4 * g + 3 * quarter * high + i % 4
            first = 2 * quarter if odd else unit
            last = unit + 2 * quarter if odd else 0
            for f, tile in enumerate((x, y)):
                ref[pl.ds(first + f * quarter + pos, 1), :] = tile[0:1]
                ref[pl.ds(last + f * quarter + pos, 1), :] = tile[7:8]
                r.first_rows[f, pl.ds(8 * g + i, 1), :] = tile[0:1]
            here = lanes == 8 * g + i
            for f, tile in enumerate((x, y)):
                cols[f] = jnp.where(here, tile[:, 0:1], cols[f])
                cols[2 + f] = jnp.where(here, tile[:, 127:128], cols[2 + f])
        return tuple(cols)

    def start_body(high, g, cols):
        flows = [(vel[8 * g + i, 0], vel[8 * g + i, 1]) for i in range(8)]
        return pack_flow(rows[0], high, g, flows, cols)

    local[1].wait()
    cols = (zero,) * 4
    turns = slots // 16
    for high in range(2):
        cols = lax.fori_loop(
            high * turns, (high + 1) * turns, functools.partial(start_body, high), cols
        )
        if high == 0:
            halo_start(early[0])
    put_cols(rows[0], cols)
    halo_start(halos[0])
    for delta in range(2, owners):
        send_share(delta)

    local[2].wait()
    local[3].wait()

    def part_body(g, c):
        made = []
        for i in range(4):
            j = 4 * g + i
            first, second = r.area_in[j, 0], r.area_in[j, 1]
            made.append((
                first + second,
                first * r.thick_in[j, 0] + second * r.thick_in[j, 1],
            ))
        for i in range(4):
            r.cover[0, 0, 4 * g + i] = made[i][0]
            r.cover[0, 1, 4 * g + i] = made[i][1]
        return c

    lax.fori_loop(0, slots // 4, part_body, 0)
    cover_copy = remote(
        r.cover.at[0], r.cover.at[1], r.cover_sems.at[0], r.cover_sems.at[1], partner
    )
    cover_copy.start()

    @pl.when(full)
    def _():
        def fill(g, c):
            tiles = [take(me * cap + 2 * g + i, range(4)) for i in range(2)]
            for i in range(2):
                for f in range(4):
                    forcing[f // 2, me * cap + 2 * g + i, f % 2] = tiles[i][f]
            return c

        lax.fori_loop(0, cap // 2, fill, 0)

    spot = lax.broadcasted_iota(jnp.int32, (128, 128), 0)
    for pick, d, toward, low in (
        (r.pick_next, 1, 1, 0),
        (r.pick_next, 4, 1, 128),
        (r.pick_prev, 3, -1, 0),
        (r.pick_prev, 5, -1, 128),
    ):
        ids = beside_ref[d : d + 1, :]
        for i in range(6):
            across, aside = i % 3 - 1, (i // 3) * toward
            base = ((me + across) * sectors + sector + aside) * slots
            hit = (ids - base == spot) & (spot < slots) & (ids >= 0)
            pick[i * 128 : (i + 1) * 128, low : low + 128] = hit.astype(f32).astype(jnp.bfloat16)

    def fetch_columns(ref, low, count, cross, pick):
        parts = [
            ref[a * unit + 4 * half + low : a * unit + 4 * half + low + count, :]
            for a in (2, 0, 3)
        ] + [cross[a] for a in range(3)]
        whole = jnp.concatenate(parts, axis=1)
        first = whole.astype(jnp.bfloat16)
        rest = whole - first.astype(f32)
        second = rest.astype(jnp.bfloat16)
        third = (rest - second.astype(f32)).astype(jnp.bfloat16)
        terms = jnp.concatenate([first, second, third], axis=0)
        got = jnp.dot(terms, pick[...], preferred_element_type=f32)
        return got[0:count] + got[count : 2 * count] + got[2 * count : 3 * count]

    local[4].wait()
    cover_copy.wait()

    def cover_body(g, cols):
        cols = list(cols)
        for part in range(2):
            made = []
            for i in range(4):
                j = 8 * g + 4 * part + i
                area = r.cover[0, 0, j] + r.cover[1, 0, j]
                volume = r.cover[0, 1, j] + r.cover[1, 1, j]
                strength = strength_scale * volume * jnp.exp(-cover_decay * (1.0 - area))
                made.append((area, volume, strength, [sig[j, f] for f in range(3)] + [strength]))
            for i, (area, volume, strength, fields) in enumerate(made):
                j = 8 * g + 4 * part + i
                r.area_buf[j] = area
                r.mass_buf[j] = volume
                r.strength_buf[j] = strength
                for f, tile in enumerate(fields):
                    r.rows_i[pl.ds(part * unit + f * half + 4 * g + i, 1), :] = tile[7:8]
                    cols[f] = jnp.where(lanes == j, tile[:, 127:128], cols[f])
        return tuple(cols)

    cols = lax.fori_loop(0, slots // 8, cover_body, (zero,) * 4)
    put_cols(r.rows_i, cols)
    halo_start(start_halo)

    def fwd_copy(s, part):
        place = forcing.at[part, pl.ds(s * cap, cap)]
        return remote(place, place, r.fwd_send.at[s], r.fwd_recv.at[s], partner)

    def ret_copy(s, o):
        return remote(
            blend.at[lev, pl.ds(s * cap, cap)],
            back.at[lev, pl.ds(o * cap, cap)],
            r.ret_send.at[s],
            r.ret_recv.at[o],
            at(s),
        )

    def ret_edge_copy(s):
        return remote(
            blend.at[:, pl.ds(s * cap - SCOLS, SCOLS)],
            back.at[:, pl.ds(blocks, SCOLS)],
            r.ret_edge.at[1 + s],
            r.ret_edge.at[0],
            at(s),
        )

    sig_copy = pltpu.make_async_copy(sig, sig_out, r.local_sems.at[4])
    vel_copy = pltpu.make_async_copy(vel, vel_out, r.local_sems.at[1])

    for sweep in range(ITERS):
        parity = sweep % 2
        ref = rows[parity]
        final = sweep == ITERS - 1
        halo_wait(early[parity])
        halo_wait(halos[parity])
        got = fetch_columns(ref, 0, 16, crossed_next[parity], r.pick_next)
        right_x, right_y = got[0:8, 0:128], got[8:16, 0:128]
        r.corner[...] = jnp.transpose(
            jnp.concatenate([got[:, 128:256], jnp.zeros((112, 128), f32)], axis=0)
        )
        got = fetch_columns(ref, 16, 16, crossed_prev[parity], r.pick_prev)
        left_x, left_y = got[0:8, 0:128], got[8:16, 0:128]
        under_x, under_y = got[0:1, 128:256], got[8:9, 128:256]

        def stress_body(g, c):
            for part in range(2):
                js = [8 * g + 4 * part + i for i in range(4)]
                last_row, last_col = subs == 7, lanes == 127
                made = []
                for j in js:
                    x, y = vel[j, 0], vel[j, 1]
                    place = row_ref[j]
                    above = row_ref[slots + j]
                    below_x = ref[pl.ds(place, 1), :]
                    below_y = ref[pl.ds(place + quarter, 1), :]
                    above_x = ref[pl.ds(above, 1), :]
                    above_y = ref[pl.ds(above + quarter, 1), :]
                    turn = 127 - j
                    new = stress_update(
                        x,
                        y,
                        jnp.where(last_row, below_x, pltpu.roll(x, 7, 0)),
                        jnp.where(last_row, below_y, pltpu.roll(y, 7, 0)),
                        jnp.where(last_col, pltpu.roll(right_x, turn, 1), pltpu.roll(x, 127, 1)),
                        jnp.where(last_col, pltpu.roll(right_y, turn, 1), pltpu.roll(y, 127, 1)),
                        sig[j, 0],
                        sig[j, 1],
                        sig[j, 2],
                        r.strength_buf[j],
                    )
                    made.append((new, above_x, above_y))
                for j, (new, above_x, above_y) in zip(js, made):
                    for f in range(3):
                        sig[j, f] = new[f]
                    r.ghost_flow[0, pl.ds(j, 1), :] = above_x
                    r.ghost_flow[1, pl.ds(j, 1), :] = above_y
            return c

        lax.fori_loop(0, slots // 8, stress_body, 0)
        if final:
            sig_copy.start()

        if sweep == 0:
            halo_wait(start_halo)
            halo_sent(start_halo)

            def gather_body(g, c):
                for i in range(8):
                    j = 8 * g + i
                    place = row_ref[2 * slots + j]
                    for f in range(4):
                        r.ghost_row[f, pl.ds(j, 1), :] = r.rows_i[pl.ds(place + f * half, 1), :]
                return c

            lax.fori_loop(0, slots // 8, gather_body, 0)
            got = fetch_columns(r.rows_i, 0, 32, r.prev_i, r.pick_prev)
            for f in range(4):
                r.ghost_col[f] = got[8 * f : 8 * f + 8, 0:128]

        own_first = [
            ref[4 * half + 8 * f : 4 * half + 8 * f + 8, :] for f in range(2)
        ]
        new = stress_update(
            left_x,
            left_y,
            jnp.where(subs == 7, under_x, pltpu.roll(left_x, 7, 0)),
            jnp.where(subs == 7, under_y, pltpu.roll(left_y, 7, 0)),
            own_first[0],
            own_first[1],
            *[r.ghost_col[f] for f in range(4)],
        )
        for f in range(3):
            r.ghost_col[f] = new[f]
        left_shear = new[2]
        left_normal = 0.5 * (new[0] - new[1])

        def ghost_body(g, c):
            made = []
            for i in range(4):
                here = pl.ds(pl.multiple_of(32 * g + 8 * i, 8), 8)
                x, y = r.ghost_flow[0, here, :], r.ghost_flow[1, here, :]
                end = r.corner[here, :]
                new = stress_update(
                    x,
                    y,
                    r.first_rows[0, here, :],
                    r.first_rows[1, here, :],
                    jnp.where(lanes == 127, end[:, 7:8], pltpu.roll(x, 127, 1)),
                    jnp.where(lanes == 127, end[:, 15:16], pltpu.roll(y, 127, 1)),
                    *[r.ghost_row[f, here, :] for f in range(4)],
                )
                made.append((here, new))
            for here, new in made:
                for f in range(3):
                    r.ghost_row[f, here, :] = new[f]
                r.upper[0, here, :] = 0.5 * (new[0] + new[1])
                r.upper[1, here, :] = new[2]
            return c

        lax.fori_loop(0, slots // 32, ghost_body, 0)
        halo_sent(early[parity])
        halo_sent(halos[parity])

        if sweep == 0:
            for s in range(chunks):

                @pl.when(me != s)
                def _():
                    out_copy(0, s).wait_recv()
                    fwd_copy(s, lev).start()

            for s in range(chunks):

                @pl.when(me != s)
                def _():
                    fwd_copy(s, 1 - lev).wait_recv()
                    fwd_copy(s, lev).wait_send()

            for s in range(1, chunks + 1):

                @pl.when(me == edge_owner(s))
                def _():
                    edge_copy(s, me).wait_recv()
                    for j in range(SCOLS):
                        for f in range(4):
                            spot_j = s * cap - SCOLS + j
                            forcing[f // 2, spot_j, f % 2] += r.edge_land[s, j, f]

        def flow_body(high, g, cols):
            here = pl.ds(pl.multiple_of(8 * g, 8), 8)
            upper_n, upper_s = r.upper[0, here, :], r.upper[1, here, :]
            flows = []
            first_row, first_col = subs == 0, lanes == 0
            for part in range(2):
                js = [8 * g + 4 * part + i for i in range(4)]
                made = []
                for i, j in enumerate(js):
                    k = 4 * part + i
                    x, y = vel[j, 0], vel[j, 1]
                    one, two, shear = sig[j, 0], sig[j, 1], sig[j, 2]
                    normal_x = 0.5 * (one + two)
                    normal_y = 0.5 * (one - two)
                    turn = jnp.where(j == 0, 0, 128 - j)
                    above_normal = jnp.where(
                        first_row, upper_n[k : k + 1], pltpu.roll(normal_x, 1, 0)
                    )
                    above_shear = jnp.where(
                        first_row, upper_s[k : k + 1], pltpu.roll(shear, 1, 0)
                    )
                    before_shear = jnp.where(
                        first_col, pltpu.roll(left_shear, turn, 1), pltpu.roll(shear, 1, 1)
                    )
                    before_normal = jnp.where(
                        first_col, pltpu.roll(left_normal, turn, 1), pltpu.roll(normal_y, 1, 1)
                    )
                    force_x = normal_x - above_normal + (shear - before_shear)
                    force_y = shear - above_shear + (normal_y - before_normal)
                    wind_x, wind_y = forcing[0, j, 0], forcing[0, j, 1]
                    cur_x, cur_y = forcing[1, j, 0], forcing[1, j, 1]
                    slip_x, slip_y = cur_x - x, cur_y - y
                    drag = jnp.sqrt(slip_x * slip_x + slip_y * slip_y + speed_floor * speed_floor)
                    mass = r.mass_buf[j]
                    heavy = mass * inertia
                    diagonal = heavy + drag
                    rotation = mass * coriolis
                    rhs_x = heavy * x + force_x + wind_x + drag * cur_x
                    rhs_y = heavy * y + force_y + wind_y + drag * cur_y
                    inverse = 1.0 / (diagonal * diagonal + rotation * rotation)
                    x = (diagonal * rhs_x + rotation * rhs_y) * inverse
                    y = (diagonal * rhs_y - rotation * rhs_x) * inverse
                    share = None
                    if final:
                        slip_x, slip_y = cur_x - x, cur_y - y
                        drag = jnp.sqrt(
                            slip_x * slip_x + slip_y * slip_y + speed_floor * speed_floor
                        )
                        area = r.area_buf[j]
                        share = (
                            area * drag * slip_x + (1.0 - area) * wind_x,
                            area * drag * slip_y + (1.0 - area) * wind_y,
                        )
                    made.append((x, y, share))
                for j, (x, y, share) in zip(js, made):
                    vel[j, 0] = x
                    vel[j, 1] = y
                    flows.append((x, y))
                    if final:
                        blend[0, j] = share[0]
                        blend[1, j] = share[1]
            if final:
                return cols
            return pack_flow(rows[1 - parity], high, g, flows, cols)

        if final:
            step = max(cap, 8)
            for low in range(0, slots, step):
                lax.fori_loop(
                    low // 8, (low + step) // 8, functools.partial(flow_body, 0), 0
                )
                for s in range(low // cap, (low + step) // cap):

                    @pl.when(me != s)
                    def _():
                        ret_copy(s, me).start()

            for s in range(1, chunks + 1):

                @pl.when(me == edge_owner(s))
                def _():
                    ret_edge_copy(s).start()

            vel_copy.start()
        else:
            cols = (zero,) * 4
            for high in range(2):
                cols = lax.fori_loop(
                    high * turns, (high + 1) * turns, functools.partial(flow_body, high), cols
                )
                if high == 0:
                    halo_start(early[1 - parity])
            put_cols(rows[1 - parity], cols)
            halo_start(halos[1 - parity])

    @pl.when(full)
    def _():
        def keep(g, c):
            tiles = [[blend[f, me * cap + 4 * g + i] for f in range(2)] for i in range(4)]
            for i in range(4):
                for f in range(2):
                    back[f, me * cap + 4 * g + i] = tiles[i][f]
            return c

        lax.fori_loop(0, cap // 4, keep, 0)

    def back_copy(o, part):
        place = back.at[part, pl.ds(o * cap, cap)]
        return remote(place, place, r.back_send.at[o], r.back_recv.at[o], partner)

    @pl.when(full)
    def _():
        for delta in range(1, owners):
            o = lax.rem(me + delta, owners)
            ret_copy(0, o).wait_recv()
            back_copy(o, lev).start()
        for delta in range(1, owners):
            o = lax.rem(me + delta, owners)
            back_copy(o, 1 - lev).wait_recv()
            back_copy(o, lev).wait_send()

    @pl.when(has_edge(me))
    def _():
        ret_edge_copy(me).wait_recv()
        edge_copy(me, edge_owner(me)).wait_send()

    def ocean_body(g, c):
        made = []
        for i in range(4):
            b = 4 * g + i
            lane = lane_ref[b]
            safe = jnp.maximum(lane, 0)
            made.append([
                jnp.where(lane >= 0, back[f, safe], ocean_ref[b, f]) for f in range(2)
            ])
        for i in range(4):
            for f in range(2):
                r.ocean_acc[4 * g + i, f] = made[i][f]
        return c

    lax.fori_loop(0, blocks // 4, ocean_body, 0)
    ocean_copy = pltpu.make_async_copy(r.ocean_acc, ocean_out, r.local_sems.at[0])
    ocean_copy.start()

    @pl.when(full)
    def _():
        for delta in range(1, owners):
            out_copy(lax.rem(me + delta, owners), me).wait_send()

    for s in range(chunks):

        @pl.when(me != s)
        def _():
            ret_copy(s, me).wait_send()

    for s in range(1, chunks + 1):

        @pl.when(me == edge_owner(s))
        def _():
            ret_edge_copy(s).wait_send()

    sig_copy.wait()
    vel_copy.wait()
    ocean_copy.wait()


def on_device(ocean_forcing, ice_home, ice_velocity, ice_stress, ice_area, ice_thick, neighbors):
    owners = lax.axis_size("blk")
    sectors = lax.axis_size("sub")
    me = lax.axis_index("blk")
    home = ice_home[0]
    blocks = ocean_forcing.shape[1]
    slots = ice_velocity.shape[1]
    cap = blocks // owners
    chunks = slots // cap
    half = slots // 2
    quarter = half // 2
    unit = 4 * half + 32

    position = lax.rem(home, slots) - me * cap
    lane = jnp.where(
        position >= 0, lax.div(home, slots) * cap + position, blocks + SCOLS + position
    )
    lane = jnp.where(home >= 0, lane, -1)
    wanted = jnp.arange(blocks + SCOLS, dtype=jnp.int32)
    ids = jnp.arange(blocks, dtype=jnp.int32)
    src = jnp.max(jnp.where(wanted[:, None] == lane[None, :], ids[None, :], -1), axis=1)

    beside = neighbors[0].T

    def places(ids, skip, own_even, own_odd, prev, following):
        across = lax.div(ids, slots * sectors) - me
        slot = lax.rem(ids, slots)
        turn = lax.div(slot, SCOLS)
        pos = lax.div(turn, 2) * SCOLS + lax.rem(slot, SCOLS)
        pos = pos + jnp.where(pos >= quarter, skip, 0)
        own = jnp.where(lax.rem(turn, 2) == 1, own_odd, own_even)
        start = jnp.where(across == 0, own, jnp.where(across < 0, prev, following))
        return jnp.where(ids >= 0, jnp.clip(start + pos, 0, 4 * unit), 4 * unit)

    rows_at = jnp.concatenate([
        places(
            beside[0], 3 * quarter, unit, 2 * quarter, 2 * unit + 2 * quarter, 3 * unit
        ),
        places(
            beside[2], 3 * quarter, 0, unit + 2 * quarter, 2 * unit, 3 * unit + 2 * quarter
        ),
        places(beside[2], 0, 0, unit, 2 * unit, 3 * unit),
    ])
    beside = jnp.pad(beside, ((0, 2), (0, 128 - slots)), constant_values=-1)

    f32 = jnp.float32
    tile = ocean_forcing.shape[3:]
    vmem = pl.BlockSpec(memory_space=pltpu.VMEM)
    smem = pl.BlockSpec(memory_space=pltpu.SMEM)
    anywhere = pl.BlockSpec(memory_space=pl.ANY)
    dma = pltpu.SemaphoreType.DMA

    def tiles(*lead):
        return pltpu.VMEM(lead + tile, f32)

    lines = 4 * unit + 3 * half + 8
    scratch = dict(
        ocean_ref=tiles(blocks, 4),
        vel=tiles(slots, 2),
        sig=tiles(slots, 3),
        area_in=tiles(slots, 2),
        thick_in=tiles(slots, 2),
        ocean_acc=tiles(blocks, 2),
        send_buf=tiles(owners, cap, 2),
        edge_send=tiles(SCOLS, 4),
        forcing=tiles(2, slots, 2),
        edge_land=tiles(chunks + 1, SCOLS, 4),
        cover=tiles(2, 2, slots),
        area_buf=tiles(slots),
        mass_buf=tiles(slots),
        strength_buf=tiles(slots),
        blend=tiles(2, slots),
        back=tiles(2, blocks + SCOLS),
        rows_0=pltpu.VMEM((lines, 128), f32),
        rows_1=pltpu.VMEM((lines, 128), f32),
        rows_i=pltpu.VMEM((lines, 128), f32),
        next_0=pltpu.VMEM((3, 16, 128), f32),
        next_1=pltpu.VMEM((3, 16, 128), f32),
        prev_0=pltpu.VMEM((3, 16, 128), f32),
        prev_1=pltpu.VMEM((3, 16, 128), f32),
        prev_i=pltpu.VMEM((3, 32, 128), f32),
        pick_next=pltpu.VMEM((6 * 128, 256), jnp.bfloat16),
        pick_prev=pltpu.VMEM((6 * 128, 256), jnp.bfloat16),
        first_rows=pltpu.VMEM((2, slots, 128), f32),
        ghost_flow=pltpu.VMEM((2, slots, 128), f32),
        ghost_row=pltpu.VMEM((4, slots, 128), f32),
        ghost_col=tiles(4),
        upper=pltpu.VMEM((2, slots, 128), f32),
        corner=pltpu.VMEM((128, 128), f32),
        local_sems=dma((5,)),
        out_send=dma((owners,)),
        out_recv=dma((owners,)),
        edge_sems=dma((chunks + 2,)),
        fwd_send=dma((chunks,)),
        fwd_recv=dma((chunks,)),
        cover_sems=dma((2,)),
        halo_send=dma((25,)),
        halo_recv=dma((25,)),
        ret_send=dma((chunks,)),
        ret_recv=dma((owners,)),
        ret_edge=dma((chunks + 2,)),
        back_send=dma((owners,)),
        back_recv=dma((owners,)),
    )
    outs = pl.pallas_call(
        functools.partial(kernel, owners, sectors),
        out_shape=(
            jax.ShapeDtypeStruct((blocks, 2) + tile, f32),
            jax.ShapeDtypeStruct((slots, 2) + tile, f32),
            jax.ShapeDtypeStruct((slots, 3) + tile, f32),
        ),
        in_specs=[smem] * 3 + [vmem] + [anywhere] * 5,
        out_specs=(anywhere,) * 3,
        scratch_shapes=[scratch[name] for name in SCRATCH],
        compiler_params=pltpu.CompilerParams(
            collective_id=0, has_side_effects=True, vmem_limit_bytes=VMEM_MB * 2**20
        ),
    )(
        src,
        lane,
        rows_at,
        beside,
        ocean_forcing[0],
        ice_velocity[0],
        ice_stress[0],
        ice_area[0],
        ice_thick[0],
    )
    return tuple(out[None] for out in outs)


def solution(mesh):
    return jax.shard_map(
        on_device,
        mesh=mesh,
        in_specs=(
            P(("groups", "sub"), "blk", None, None, None),
            P(("groups", "sub"), "blk"),
            P(("groups", "sub"), "blk", None, None, None),
            P(("groups", "sub"), "blk", None, None, None),
            P(("groups", "sub"), "blk", "lev", None, None),
            P(("groups", "sub"), "blk", "lev", None, None),
            P(("groups", "sub"), "blk", None),
        ),
        out_specs=(
            P(("groups", "sub"), "blk", None, None, None),
            P(("groups", "sub"), "blk", None, None, None),
            P(("groups", "sub"), "blk", None, None, None),
        ),
        check_vma=False,
    )
```

```python
import functools
import types

import jax
import jax.numpy as jnp
from jax import lax
from jax.experimental import pallas as pl
from jax.experimental.pallas import tpu as pltpu
from jax.sharding import PartitionSpec as P

SCOLS = 4
ITERS = 4
VMEM_MB = 60

strength_scale = 4.0
cover_decay = 4.0
elastic_weight = 1.0
ellipse_square = 4.0
delta_floor = 0.05
inertia = 2.0
speed_floor = 0.2
coriolis = 0.6

MESH = pl.DeviceIdType.MESH


SCRATCH = (
    "ocean_ref", "vel", "sig", "area_in", "thick_in", "ocean_acc", "send_buf", "edge_send",
    "forcing", "edge_land", "cover", "area_buf", "mass_buf", "strength_buf", "blend", "back",
    "rows_0", "rows_1", "rows_i", "next_0", "next_1", "prev_0", "prev_1", "prev_i", "pick_next",
    "pick_prev", "first_rows", "ghost_flow", "ghost_row", "ghost_col", "upper", "corner",
    "local_sems", "out_send", "out_recv", "edge_sems", "fwd_send", "fwd_recv", "cover_sems",
    "halo_send", "halo_recv", "ret_send", "ret_recv", "ret_edge", "back_send", "back_recv",
)


def stress_update(flow_x, flow_y, down_x, down_y, right_x, right_y, one, two, shear, strength):
    stretch_x = down_x - flow_x
    stretch_y = right_y - flow_y
    shear_rate = right_x - flow_x + (down_y - flow_y)
    divergence = stretch_x + stretch_y
    tension = stretch_x - stretch_y
    square = (
        divergence * divergence
        + (tension * tension + shear_rate * shear_rate) * (1.0 / ellipse_square)
        + delta_floor * delta_floor
    )
    weight = elastic_weight * strength * lax.rsqrt(square)
    relax = 1.0 / (1.0 + elastic_weight)
    return (
        (one + weight * divergence - elastic_weight * strength) * relax,
        (two + weight * tension * (1.0 / ellipse_square)) * relax,
        (shear + weight * shear_rate * (0.5 / ellipse_square)) * relax,
    )


def kernel(owners, sectors, *refs):
    (
        src_ref,
        lane_ref,
        row_ref,
        beside_ref,
        ocean_hbm,
        vel_hbm,
        stress_hbm,
        area_hbm,
        thick_hbm,
        ocean_out,
        vel_out,
        sig_out,
    ) = refs[:12]
    r = types.SimpleNamespace(**dict(zip(SCRATCH, refs[12:], strict=True)))
    group = lax.axis_index("groups")
    me = lax.axis_index("blk")
    sector = lax.axis_index("sub")
    lev = lax.axis_index("lev")
    ocean_ref, vel, sig, forcing, blend, back = (
        r.ocean_ref, r.vel, r.sig, r.forcing, r.blend, r.back
    )
    slots = vel.shape[0]
    blocks = ocean_ref.shape[0]
    cap = blocks // owners
    chunks = slots // cap
    half = slots // 2
    quarter = half // 2
    unit = 4 * half + 32
    f32 = jnp.float32

    def at(blk, sub=None, core=None):
        return (
            group,
            blk,
            sector if sub is None else sub,
            lev if core is None else core,
        )

    partner = at(me, None, 1 - lev)

    def remote(src, dst, send, recv, target):
        return pltpu.make_async_remote_copy(
            src_ref=src,
            dst_ref=dst,
            send_sem=send,
            recv_sem=recv,
            device_id=target,
            device_id_type=MESH,
        )

    local = [
        pltpu.make_async_copy(src, dst, r.local_sems.at[i])
        for i, (src, dst) in enumerate((
            (ocean_hbm, ocean_ref),
            (vel_hbm, vel),
            (area_hbm, r.area_in),
            (thick_hbm, r.thick_in),
            (stress_hbm, sig),
        ))
    ]
    for copy in local:
        copy.start()

    lanes = lax.broadcasted_iota(jnp.int32, (8, 128), 1)
    subs = lax.broadcasted_iota(jnp.int32, (8, 128), 0)
    zero = jnp.zeros((8, 128), f32)

    rows = (r.rows_0, r.rows_1)
    crossed_next = (r.next_0, r.next_1)
    crossed_prev = (r.prev_0, r.prev_1)
    for ref in (*rows, r.rows_i):
        for a in (2, 3):
            ref[a * unit + 4 * half : (a + 1) * unit, :] = jnp.zeros((32, 128), f32)
        rest = ref.shape[0] - 4 * unit
        ref[4 * unit :, :] = jnp.zeros((rest, 128), f32)
    for ref in (*crossed_next, *crossed_prev, r.prev_i):
        ref[...] = jnp.zeros(ref.shape, f32)

    barrier = pltpu.get_barrier_semaphore()

    def greet(target):
        pl.semaphore_signal(barrier, inc=1, device_id=target, device_id_type=MESH)

    greet(partner)
    for delta in range(1, owners):
        greet(at(lax.rem(me + delta, owners)))
    expected = owners
    for ds in (-1, 1):
        for da in (-1, 0, 1):
            q, o = sector + ds, me + da
            ok = (q >= 0) & (q < sectors) & (o >= 0) & (o < owners)

            @pl.when(ok)
            def _():
                greet(at(o, q))

            expected = expected + ok.astype(jnp.int32)
    local[0].wait()
    pl.semaphore_wait(barrier, expected)

    def out_copy(o, s):
        return remote(
            r.send_buf.at[o],
            forcing.at[lev, pl.ds(s * cap, cap)],
            r.out_send.at[o],
            r.out_recv.at[s],
            at(o),
        )

    full = me * cap < slots

    def take(lane, fields):
        src = src_ref[lane]
        safe = jnp.maximum(src, 0)
        return [jnp.where(src >= 0, ocean_ref[safe, f], 0.0) for f in fields]

    def send_share(delta):
        o = lax.rem(me + delta, owners)

        @pl.when(full)
        def _():
            def fill(g, c):
                tiles = [take(o * cap + 4 * g + i, (2 * lev, 2 * lev + 1)) for i in range(4)]
                for i in range(4):
                    for f in range(2):
                        r.send_buf[o, 4 * g + i, f] = tiles[i][f]
                return c

            lax.fori_loop(0, cap // 4, fill, 0)
            out_copy(o, me).start()

    send_share(1)

    def edge_owner(s):
        last_pass = s * (cap // SCOLS) - 1
        return jnp.where(lax.rem(last_pass + 2, 2) == 0, owners - 1, 0)

    def has_edge(s):
        return (s >= 1) & (s <= chunks)

    def edge_copy(s, o):
        return remote(
            r.edge_send, r.edge_land.at[s], r.edge_sems.at[0], r.edge_sems.at[1 + s], at(o)
        )

    @pl.when(has_edge(me))
    def _():
        for j in range(SCOLS):
            tiles = take(blocks + j, range(4))
            for f in range(4):
                r.edge_send[j, f] = tiles[f]
        edge_copy(me, edge_owner(me)).start()

    def line_copies(ref, base, low=0, high=unit):
        count = high - low
        return [
            (me + 1 < owners, remote(
                ref.at[pl.ds(low, count)], ref.at[pl.ds(2 * unit + low, count)],
                r.halo_send.at[base], r.halo_recv.at[base], at(me + 1)), me >= 1),
            (me >= 1, remote(
                ref.at[pl.ds(unit + low, count)], ref.at[pl.ds(3 * unit + low, count)],
                r.halo_send.at[base + 1], r.halo_recv.at[base + 1], at(me - 1)),
                me + 1 < owners),
        ]

    def cross_copies(cols, cross, down, base):
        target, source = sector + down, sector - down
        t_ok = (target >= 0) & (target < sectors)
        s_ok = (source >= 0) & (source < sectors)
        made = []
        for i, da in enumerate((1, 0, -1)):
            o, p = me + da, me - da
            made.append((t_ok & (o >= 0) & (o < owners), remote(
                cols, cross.at[1 - da], r.halo_send.at[base + i], r.halo_recv.at[base + i],
                at(o, target)), s_ok & (p >= 0) & (p < owners)))
        return made

    def halo_copies(parity):
        ref, base = rows[parity], 10 * parity
        first = ref.at[pl.ds(4 * half, 16)]
        last = ref.at[pl.ds(4 * half + 16, 16)]
        return (
            cross_copies(first, crossed_next[parity], -1, base + 2)
            + cross_copies(last, crossed_prev[parity], 1, base + 5)
            + line_copies(ref, base, 2 * half, unit)
        )

    def early_copies(parity):
        return line_copies(rows[parity], 10 * parity + 8, 0, 2 * half)

    early = [early_copies(0), early_copies(1)]
    halos = [halo_copies(0), halo_copies(1)]
    start_halo = cross_copies(
        r.rows_i.at[pl.ds(4 * half, 32)], r.prev_i, 1, 22
    ) + line_copies(r.rows_i, 20)

    def halo_start(copies):
        for ok, copy, _ in copies:
            pl.when(ok)(copy.start)

    def halo_wait(copies):
        for _, copy, arriving in copies:
            pl.when(arriving)(copy.wait_recv)

    def halo_sent(copies):
        for ok, copy, _ in copies:
            pl.when(ok)(copy.wait_send)

    def put_cols(ref, cols):
        for i, col in enumerate(cols):
            for a in range(2):
                low = a * unit + 4 * half + 8 * i
                ref[low : low + 8, :] = col

    def pack_flow(ref, high, g, flows, cols):
        cols = list(cols)
        for i, (x, y) in enumerate(flows):
            odd, pos = i // 4, 4 * g + 3 * quarter * high + i % 4
            first = 2 * quarter if odd else unit
            last = unit + 2 * quarter if odd else 0
            for f, tile in enumerate((x, y)):
                ref[pl.ds(first + f * quarter + pos, 1), :] = tile[0:1]
                ref[pl.ds(last + f * quarter + pos, 1), :] = tile[7:8]
                r.first_rows[f, pl.ds(8 * g + i, 1), :] = tile[0:1]
            here = lanes == 8 * g + i
            for f, tile in enumerate((x, y)):
                cols[f] = jnp.where(here, tile[:, 0:1], cols[f])
                cols[2 + f] = jnp.where(here, tile[:, 127:128], cols[2 + f])
        return tuple(cols)

    def start_body(high, g, cols):
        flows = [(vel[8 * g + i, 0], vel[8 * g + i, 1]) for i in range(8)]
        return pack_flow(rows[0], high, g, flows, cols)

    local[1].wait()
    cols = (zero,) * 4
    turns = slots // 16
    for high in range(2):
        cols = lax.fori_loop(
            high * turns, (high + 1) * turns, functools.partial(start_body, high), cols
        )
        if high == 0:
            halo_start(early[0])
    put_cols(rows[0], cols)
    halo_start(halos[0])
    for delta in range(2, owners):
        send_share(delta)

    local[2].wait()
    local[3].wait()

    def part_body(g, c):
        made = []
        for i in range(4):
            j = 4 * g + i
            first, second = r.area_in[j, 0], r.area_in[j, 1]
            made.append((
                first + second,
                first * r.thick_in[j, 0] + second * r.thick_in[j, 1],
            ))
        for i in range(4):
            r.cover[0, 0, 4 * g + i] = made[i][0]
            r.cover[0, 1, 4 * g + i] = made[i][1]
        return c

    lax.fori_loop(0, slots // 4, part_body, 0)
    cover_copy = remote(
        r.cover.at[0], r.cover.at[1], r.cover_sems.at[0], r.cover_sems.at[1], partner
    )
    cover_copy.start()

    @pl.when(full)
    def _():
        def fill(g, c):
            tiles = [take(me * cap + 2 * g + i, range(4)) for i in range(2)]
            for i in range(2):
                for f in range(4):
                    forcing[f // 2, me * cap + 2 * g + i, f % 2] = tiles[i][f]
            return c

        lax.fori_loop(0, cap // 2, fill, 0)

    spot = lax.broadcasted_iota(jnp.int32, (128, slots), 0)
    for pick in (r.pick_next, r.pick_prev):
        pick[...] = jnp.zeros(pick.shape, jnp.bfloat16)
    for pick, d, toward, low in (
        (r.pick_next, 1, 1, 0),
        (r.pick_next, 4, 1, 128),
        (r.pick_prev, 3, -1, 0),
        (r.pick_prev, 5, -1, 128),
    ):
        ids = beside_ref[d : d + 1, :]
        for i in range(6):
            across, aside = i % 3 - 1, (i // 3) * toward
            base = ((me + across) * sectors + sector + aside) * slots
            hit = (ids - base == spot) & (spot < slots) & (ids >= 0)
            pick[i * 128 : (i + 1) * 128, low : low + slots] = hit.astype(f32).astype(jnp.bfloat16)

    def fetch_columns(ref, low, count, cross, pick):
        parts = [
            ref[a * unit + 4 * half + low : a * unit + 4 * half + low + count, :]
            for a in (2, 0, 3)
        ] + [cross[a] for a in range(3)]
        whole = jnp.concatenate(parts, axis=1)
        first = whole.astype(jnp.bfloat16)
        rest = whole - first.astype(f32)
        second = rest.astype(jnp.bfloat16)
        third = (rest - second.astype(f32)).astype(jnp.bfloat16)
        terms = jnp.concatenate([first, second, third], axis=0)
        got = jnp.dot(terms, pick[...], preferred_element_type=f32)
        return got[0:count] + got[count : 2 * count] + got[2 * count : 3 * count]

    local[4].wait()
    cover_copy.wait()

    def cover_body(g, cols):
        cols = list(cols)
        for part in range(2):
            made = []
            for i in range(4):
                j = 8 * g + 4 * part + i
                area = r.cover[0, 0, j] + r.cover[1, 0, j]
                volume = r.cover[0, 1, j] + r.cover[1, 1, j]
                strength = strength_scale * volume * jnp.exp(-cover_decay * (1.0 - area))
                made.append((area, volume, strength, [sig[j, f] for f in range(3)] + [strength]))
            for i, (area, volume, strength, fields) in enumerate(made):
                j = 8 * g + 4 * part + i
                r.area_buf[j] = area
                r.mass_buf[j] = volume
                r.strength_buf[j] = strength
                for f, tile in enumerate(fields):
                    r.rows_i[pl.ds(part * unit + f * half + 4 * g + i, 1), :] = tile[7:8]
                    cols[f] = jnp.where(lanes == j, tile[:, 127:128], cols[f])
        return tuple(cols)

    cols = lax.fori_loop(0, slots // 8, cover_body, (zero,) * 4)
    put_cols(r.rows_i, cols)
    halo_start(start_halo)

    def fwd_copy(s, part):
        place = forcing.at[part, pl.ds(s * cap, cap)]
        return remote(place, place, r.fwd_send.at[s], r.fwd_recv.at[s], partner)

    def ret_copy(s, o):
        return remote(
            blend.at[lev, pl.ds(s * cap, cap)],
            back.at[lev, pl.ds(o * cap, cap)],
            r.ret_send.at[s],
            r.ret_recv.at[o],
            at(s),
        )

    def ret_edge_copy(s):
        return remote(
            blend.at[:, pl.ds(s * cap - SCOLS, SCOLS)],
            back.at[:, pl.ds(blocks, SCOLS)],
            r.ret_edge.at[1 + s],
            r.ret_edge.at[0],
            at(s),
        )

    sig_copy = pltpu.make_async_copy(sig, sig_out, r.local_sems.at[4])
    vel_copy = pltpu.make_async_copy(vel, vel_out, r.local_sems.at[1])

    for sweep in range(ITERS):
        parity = sweep % 2
        ref = rows[parity]
        final = sweep == ITERS - 1
        halo_wait(early[parity])
        halo_wait(halos[parity])
        got = fetch_columns(ref, 0, 16, crossed_next[parity], r.pick_next)
        right_x, right_y = got[0:8, 0:128], got[8:16, 0:128]
        r.corner[...] = jnp.transpose(
            jnp.concatenate([got[:, 128:256], jnp.zeros((112, 128), f32)], axis=0)
        )
        got = fetch_columns(ref, 16, 16, crossed_prev[parity], r.pick_prev)
        left_x, left_y = got[0:8, 0:128], got[8:16, 0:128]
        under_x, under_y = got[0:1, 128:256], got[8:9, 128:256]

        def stress_body(g, c):
            for part in range(2):
                js = [8 * g + 4 * part + i for i in range(4)]
                last_row, last_col = subs == 7, lanes == 127
                made = []
                for j in js:
                    x, y = vel[j, 0], vel[j, 1]
                    place = row_ref[j]
                    above = row_ref[slots + j]
                    below_x = ref[pl.ds(place, 1), :]
                    below_y = ref[pl.ds(place + quarter, 1), :]
                    above_x = ref[pl.ds(above, 1), :]
                    above_y = ref[pl.ds(above + quarter, 1), :]
                    turn = 127 - j
                    new = stress_update(
                        x,
                        y,
                        jnp.where(last_row, below_x, pltpu.roll(x, 7, 0)),
                        jnp.where(last_row, below_y, pltpu.roll(y, 7, 0)),
                        jnp.where(last_col, pltpu.roll(right_x, turn, 1), pltpu.roll(x, 127, 1)),
                        jnp.where(last_col, pltpu.roll(right_y, turn, 1), pltpu.roll(y, 127, 1)),
                        sig[j, 0],
                        sig[j, 1],
                        sig[j, 2],
                        r.strength_buf[j],
                    )
                    made.append((new, above_x, above_y))
                for j, (new, above_x, above_y) in zip(js, made):
                    for f in range(3):
                        sig[j, f] = new[f]
                    r.ghost_flow[0, pl.ds(j, 1), :] = above_x
                    r.ghost_flow[1, pl.ds(j, 1), :] = above_y
            return c

        lax.fori_loop(0, slots // 8, stress_body, 0)
        if final:
            sig_copy.start()

        if sweep == 0:
            halo_wait(start_halo)
            halo_sent(start_halo)

            def gather_body(g, c):
                for i in range(8):
                    j = 8 * g + i
                    place = row_ref[2 * slots + j]
                    for f in range(4):
                        r.ghost_row[f, pl.ds(j, 1), :] = r.rows_i[pl.ds(place + f * half, 1), :]
                return c

            lax.fori_loop(0, slots // 8, gather_body, 0)
            got = fetch_columns(r.rows_i, 0, 32, r.prev_i, r.pick_prev)
            for f in range(4):
                r.ghost_col[f] = got[8 * f : 8 * f + 8, 0:128]

        own_first = [
            ref[4 * half + 8 * f : 4 * half + 8 * f + 8, :] for f in range(2)
        ]
        new = stress_update(
            left_x,
            left_y,
            jnp.where(subs == 7, under_x, pltpu.roll(left_x, 7, 0)),
            jnp.where(subs == 7, under_y, pltpu.roll(left_y, 7, 0)),
            own_first[0],
            own_first[1],
            *[r.ghost_col[f] for f in range(4)],
        )
        for f in range(3):
            r.ghost_col[f] = new[f]
        left_shear = new[2]
        left_normal = 0.5 * (new[0] - new[1])

        def ghost_body(g, c):
            made = []
            for i in range(4):
                here = pl.ds(pl.multiple_of(32 * g + 8 * i, 8), 8)
                x, y = r.ghost_flow[0, here, :], r.ghost_flow[1, here, :]
                end = r.corner[here, :]
                new = stress_update(
                    x,
                    y,
                    r.first_rows[0, here, :],
                    r.first_rows[1, here, :],
                    jnp.where(lanes == 127, end[:, 7:8], pltpu.roll(x, 127, 1)),
                    jnp.where(lanes == 127, end[:, 15:16], pltpu.roll(y, 127, 1)),
                    *[r.ghost_row[f, here, :] for f in range(4)],
                )
                made.append((here, new))
            for here, new in made:
                for f in range(3):
                    r.ghost_row[f, here, :] = new[f]
                r.upper[0, here, :] = 0.5 * (new[0] + new[1])
                r.upper[1, here, :] = new[2]
            return c

        lax.fori_loop(0, slots // 32, ghost_body, 0)
        halo_sent(early[parity])
        halo_sent(halos[parity])

        if sweep == 0:
            for s in range(chunks):

                @pl.when(me != s)
                def _():
                    out_copy(0, s).wait_recv()
                    fwd_copy(s, lev).start()

            for s in range(chunks):

                @pl.when(me != s)
                def _():
                    fwd_copy(s, 1 - lev).wait_recv()
                    fwd_copy(s, lev).wait_send()

            for s in range(1, chunks + 1):

                @pl.when(me == edge_owner(s))
                def _():
                    edge_copy(s, me).wait_recv()
                    for j in range(SCOLS):
                        for f in range(4):
                            spot_j = s * cap - SCOLS + j
                            forcing[f // 2, spot_j, f % 2] += r.edge_land[s, j, f]

        def flow_body(high, g, cols):
            here = pl.ds(pl.multiple_of(8 * g, 8), 8)
            upper_n, upper_s = r.upper[0, here, :], r.upper[1, here, :]
            flows = []
            first_row, first_col = subs == 0, lanes == 0
            for part in range(2):
                js = [8 * g + 4 * part + i for i in range(4)]
                made = []
                for i, j in enumerate(js):
                    k = 4 * part + i
                    x, y = vel[j, 0], vel[j, 1]
                    one, two, shear = sig[j, 0], sig[j, 1], sig[j, 2]
                    normal_x = 0.5 * (one + two)
                    normal_y = 0.5 * (one - two)
                    turn = jnp.where(j == 0, 0, 128 - j)
                    above_normal = jnp.where(
                        first_row, upper_n[k : k + 1], pltpu.roll(normal_x, 1, 0)
                    )
                    above_shear = jnp.where(
                        first_row, upper_s[k : k + 1], pltpu.roll(shear, 1, 0)
                    )
                    before_shear = jnp.where(
                        first_col, pltpu.roll(left_shear, turn, 1), pltpu.roll(shear, 1, 1)
                    )
                    before_normal = jnp.where(
                        first_col, pltpu.roll(left_normal, turn, 1), pltpu.roll(normal_y, 1, 1)
                    )
                    force_x = normal_x - above_normal + (shear - before_shear)
                    force_y = shear - above_shear + (normal_y - before_normal)
                    wind_x, wind_y = forcing[0, j, 0], forcing[0, j, 1]
                    cur_x, cur_y = forcing[1, j, 0], forcing[1, j, 1]
                    slip_x, slip_y = cur_x - x, cur_y - y
                    drag = jnp.sqrt(slip_x * slip_x + slip_y * slip_y + speed_floor * speed_floor)
                    mass = r.mass_buf[j]
                    heavy = mass * inertia
                    diagonal = heavy + drag
                    rotation = mass * coriolis
                    rhs_x = heavy * x + force_x + wind_x + drag * cur_x
                    rhs_y = heavy * y + force_y + wind_y + drag * cur_y
                    inverse = 1.0 / (diagonal * diagonal + rotation * rotation)
                    x = (diagonal * rhs_x + rotation * rhs_y) * inverse
                    y = (diagonal * rhs_y - rotation * rhs_x) * inverse
                    share = None
                    if final:
                        slip_x, slip_y = cur_x - x, cur_y - y
                        drag = jnp.sqrt(
                            slip_x * slip_x + slip_y * slip_y + speed_floor * speed_floor
                        )
                        area = r.area_buf[j]
                        share = (
                            area * drag * slip_x + (1.0 - area) * wind_x,
                            area * drag * slip_y + (1.0 - area) * wind_y,
                        )
                    made.append((x, y, share))
                for j, (x, y, share) in zip(js, made):
                    vel[j, 0] = x
                    vel[j, 1] = y
                    flows.append((x, y))
                    if final:
                        blend[0, j] = share[0]
                        blend[1, j] = share[1]
            if final:
                return cols
            return pack_flow(rows[1 - parity], high, g, flows, cols)

        if final:
            step = max(cap, 8)
            for low in range(0, slots, step):
                lax.fori_loop(
                    low // 8, (low + step) // 8, functools.partial(flow_body, 0), 0
                )
                for s in range(low // cap, (low + step) // cap):

                    @pl.when(me != s)
                    def _():
                        ret_copy(s, me).start()

            for s in range(1, chunks + 1):

                @pl.when(me == edge_owner(s))
                def _():
                    ret_edge_copy(s).start()

            vel_copy.start()
        else:
            cols = (zero,) * 4
            for high in range(2):
                cols = lax.fori_loop(
                    high * turns, (high + 1) * turns, functools.partial(flow_body, high), cols
                )
                if high == 0:
                    halo_start(early[1 - parity])
            put_cols(rows[1 - parity], cols)
            halo_start(halos[1 - parity])

    @pl.when(full)
    def _():
        def keep(g, c):
            tiles = [[blend[f, me * cap + 4 * g + i] for f in range(2)] for i in range(4)]
            for i in range(4):
                for f in range(2):
                    back[f, me * cap + 4 * g + i] = tiles[i][f]
            return c

        lax.fori_loop(0, cap // 4, keep, 0)

    def back_copy(o, part):
        place = back.at[part, pl.ds(o * cap, cap)]
        return remote(place, place, r.back_send.at[o], r.back_recv.at[o], partner)

    @pl.when(full)
    def _():
        for delta in range(1, owners):
            o = lax.rem(me + delta, owners)
            ret_copy(0, o).wait_recv()
            back_copy(o, lev).start()
        for delta in range(1, owners):
            o = lax.rem(me + delta, owners)
            back_copy(o, 1 - lev).wait_recv()
            back_copy(o, lev).wait_send()

    @pl.when(has_edge(me))
    def _():
        ret_edge_copy(me).wait_recv()
        edge_copy(me, edge_owner(me)).wait_send()

    def ocean_body(g, c):
        made = []
        for i in range(4):
            b = 4 * g + i
            lane = lane_ref[b]
            safe = jnp.maximum(lane, 0)
            made.append([
                jnp.where(lane >= 0, back[f, safe], ocean_ref[b, f]) for f in range(2)
            ])
        for i in range(4):
            for f in range(2):
                r.ocean_acc[4 * g + i, f] = made[i][f]
        return c

    lax.fori_loop(0, blocks // 4, ocean_body, 0)
    ocean_copy = pltpu.make_async_copy(r.ocean_acc, ocean_out, r.local_sems.at[0])
    ocean_copy.start()

    @pl.when(full)
    def _():
        for delta in range(1, owners):
            out_copy(lax.rem(me + delta, owners), me).wait_send()

    for s in range(chunks):

        @pl.when(me != s)
        def _():
            ret_copy(s, me).wait_send()

    for s in range(1, chunks + 1):

        @pl.when(me == edge_owner(s))
        def _():
            ret_edge_copy(s).wait_send()

    sig_copy.wait()
    vel_copy.wait()
    ocean_copy.wait()


def on_device(ocean_forcing, ice_home, ice_velocity, ice_stress, ice_area, ice_thick, neighbors):
    owners = lax.axis_size("blk")
    sectors = lax.axis_size("sub")
    me = lax.axis_index("blk")
    home = ice_home[0]
    blocks = ocean_forcing.shape[1]
    slots = ice_velocity.shape[1]
    cap = blocks // owners
    chunks = slots // cap
    half = slots // 2
    quarter = half // 2
    unit = 4 * half + 32

    position = lax.rem(home, slots) - me * cap
    lane = jnp.where(
        position >= 0, lax.div(home, slots) * cap + position, blocks + SCOLS + position
    )
    lane = jnp.where(home >= 0, lane, -1)
    wanted = jnp.arange(blocks + SCOLS, dtype=jnp.int32)
    ids = jnp.arange(blocks, dtype=jnp.int32)
    src = jnp.max(jnp.where(wanted[:, None] == lane[None, :], ids[None, :], -1), axis=1)

    beside = neighbors[0].T

    def places(ids, skip, own_even, own_odd, prev, following):
        across = lax.div(ids, slots * sectors) - me
        slot = lax.rem(ids, slots)
        turn = lax.div(slot, SCOLS)
        pos = lax.div(turn, 2) * SCOLS + lax.rem(slot, SCOLS)
        pos = pos + jnp.where(pos >= quarter, skip, 0)
        own = jnp.where(lax.rem(turn, 2) == 1, own_odd, own_even)
        start = jnp.where(across == 0, own, jnp.where(across < 0, prev, following))
        return jnp.where(ids >= 0, jnp.clip(start + pos, 0, 4 * unit), 4 * unit)

    rows_at = jnp.concatenate([
        places(
            beside[0], 3 * quarter, unit, 2 * quarter, 2 * unit + 2 * quarter, 3 * unit
        ),
        places(
            beside[2], 3 * quarter, 0, unit + 2 * quarter, 2 * unit, 3 * unit + 2 * quarter
        ),
        places(beside[2], 0, 0, unit, 2 * unit, 3 * unit),
    ])

    f32 = jnp.float32
    tile = ocean_forcing.shape[3:]
    vmem = pl.BlockSpec(memory_space=pltpu.VMEM)
    smem = pl.BlockSpec(memory_space=pltpu.SMEM)
    anywhere = pl.BlockSpec(memory_space=pl.ANY)
    dma = pltpu.SemaphoreType.DMA

    def tiles(*lead):
        return pltpu.VMEM(lead + tile, f32)

    lines = 4 * unit + 3 * half + 8
    scratch = dict(
        ocean_ref=tiles(blocks, 4),
        vel=tiles(slots, 2),
        sig=tiles(slots, 3),
        area_in=tiles(slots, 2),
        thick_in=tiles(slots, 2),
        ocean_acc=tiles(blocks, 2),
        send_buf=tiles(owners, cap, 2),
        edge_send=tiles(SCOLS, 4),
        forcing=tiles(2, slots, 2),
        edge_land=tiles(chunks + 1, SCOLS, 4),
        cover=tiles(2, 2, slots),
        area_buf=tiles(slots),
        mass_buf=tiles(slots),
        strength_buf=tiles(slots),
        blend=tiles(2, slots),
        back=tiles(2, blocks + SCOLS),
        rows_0=pltpu.VMEM((lines, 128), f32),
        rows_1=pltpu.VMEM((lines, 128), f32),
        rows_i=pltpu.VMEM((lines, 128), f32),
        next_0=pltpu.VMEM((3, 16, 128), f32),
        next_1=pltpu.VMEM((3, 16, 128), f32),
        prev_0=pltpu.VMEM((3, 16, 128), f32),
        prev_1=pltpu.VMEM((3, 16, 128), f32),
        prev_i=pltpu.VMEM((3, 32, 128), f32),
        pick_next=pltpu.VMEM((6 * 128, 256), jnp.bfloat16),
        pick_prev=pltpu.VMEM((6 * 128, 256), jnp.bfloat16),
        first_rows=pltpu.VMEM((2, slots, 128), f32),
        ghost_flow=pltpu.VMEM((2, slots, 128), f32),
        ghost_row=pltpu.VMEM((4, slots, 128), f32),
        ghost_col=tiles(4),
        upper=pltpu.VMEM((2, slots, 128), f32),
        corner=pltpu.VMEM((128, 128), f32),
        local_sems=dma((5,)),
        out_send=dma((owners,)),
        out_recv=dma((owners,)),
        edge_sems=dma((chunks + 2,)),
        fwd_send=dma((chunks,)),
        fwd_recv=dma((chunks,)),
        cover_sems=dma((2,)),
        halo_send=dma((25,)),
        halo_recv=dma((25,)),
        ret_send=dma((chunks,)),
        ret_recv=dma((owners,)),
        ret_edge=dma((chunks + 2,)),
        back_send=dma((owners,)),
        back_recv=dma((owners,)),
    )
    outs = pl.pallas_call(
        functools.partial(kernel, owners, sectors),
        out_shape=(
            jax.ShapeDtypeStruct((blocks, 2) + tile, f32),
            jax.ShapeDtypeStruct((slots, 2) + tile, f32),
            jax.ShapeDtypeStruct((slots, 3) + tile, f32),
        ),
        in_specs=[smem] * 3 + [vmem] + [anywhere] * 5,
        out_specs=(anywhere,) * 3,
        scratch_shapes=[scratch[name] for name in SCRATCH],
        compiler_params=pltpu.CompilerParams(
            collective_id=0, has_side_effects=True, vmem_limit_bytes=VMEM_MB * 2**20
        ),
    )(
        src,
        lane,
        rows_at,
        beside,
        ocean_forcing[0],
        ice_velocity[0],
        ice_stress[0],
        ice_area[0],
        ice_thick[0],
    )
    return tuple(out[None] for out in outs)


def solution(mesh):
    return jax.shard_map(
        on_device,
        mesh=mesh,
        in_specs=(
            P(("groups", "sub"), "blk", None, None, None),
            P(("groups", "sub"), "blk"),
            P(("groups", "sub"), "blk", None, None, None),
            P(("groups", "sub"), "blk", None, None, None),
            P(("groups", "sub"), "blk", "lev", None, None),
            P(("groups", "sub"), "blk", "lev", None, None),
            P(("groups", "sub"), "blk", None),
        ),
        out_specs=(
            P(("groups", "sub"), "blk", None, None, None),
            P(("groups", "sub"), "blk", None, None, None),
            P(("groups", "sub"), "blk", None, None, None),
        ),
        check_vma=False,
    )
```
